32 devices in a mesh: seq: 8 (over y, x, core), grp: 4 (over z).
Axes of the slice: x: 2, y: 2, z: 4, core: 2. Of those that a mesh axis runs over, the one named last changes fastest.
Arguments:
- tokens: bfloat16 [1024, 16, 2048], P('grp', 'seq'), may hold values from -6 to 6
- norm_gain: float32 [2048], replicated, may hold values from 0.25 to 1.75
- qk_gain: float32 [2, 2, 16, 128], P(None, None, 'grp'), may hold values from 0.5 to 12
- window_blocks: int32 [8, 4], replicated, may hold values from 0 to 7, as said below
- w_spatial: bfloat16 [2048, 3, 2048], P('seq', None, 'grp'), may hold values from -0.13258252 to 0.13258252
- w_temporal: bfloat16 [2048, 3, 2048], P('seq', None, 'grp'), may hold values from -0.13258252 to 0.13258252
- w_out: bfloat16 [2048, 2, 2048], P('seq', None, 'grp'), may hold values from -0.09375 to 0.09375
Outputs:
- block_out: bfloat16 [1024, 16, 2048], P('grp', 'seq')
The draws below stay inside these ranges and needn't reach their ends.
Inputs may be any that keep to these rules, and one draw needn't show every extreme that they name: `window_blocks`: row t lists 4 distinct tiles, the first of them t itself.
All inputs are finite; a program needn't handle non-finite values.
Results may differ from the reference program's by a relative error of at most 0.015.
Values may be sent and summed in bfloat16 or wider, within the bound.
No kernel may reach another device: no remote copies, remote signals or barrier semaphores. Data moves between devices by JAX's collectives and lax.ppermute only.
A program may use at most 128 MiB of HBM per device.

```python
import jax
import jax.numpy as jnp
from jax import lax

D = 2048
HEADS = 16
HD = 128
P_SIZE = 1024
TILE = 128
NB = 4
F = 16
HEADS_DEV = 4
NT = 8
N_GRP = 4


def attention_weight(key, marker):
    column_count = HEADS * HD
    base_draw = jnp.clip(jax.random.normal(jax.random.fold_in(key, marker), (D, 3, column_count), jnp.float32), -6.0, 6.0)
    return (base_draw * D ** (-0.5)).astype(jnp.bfloat16)


def draw_w_spatial(key, part):
    return attention_weight(key, 11)


def draw_w_temporal(key, part):
    return attention_weight(key, 23)


def draw_qk_gain(key, part):
    return jax.random.uniform(jax.random.fold_in(key, 33), (2, 2, HEADS, HD), jnp.float32, 0.5, 2.0)


def draw_window_blocks(key, part):
    row_keys = jax.random.split(jax.random.fold_in(key, 41), NT)

    def one_row(row_key, own_tile):
        others = jax.random.permutation(row_key, NT - 1)[:NB - 1]
        return jnp.concatenate([own_tile[None], (own_tile + 1 + others) % NT]).astype(jnp.int32)
    return jax.vmap(one_row)(row_keys, jnp.arange(NT, dtype=jnp.int32))


def block_scale(stream_key, dims, pieces, smallest, top_value):
    def one(dim, parts):
        heights = jax.random.uniform(jax.random.fold_in(jax.random.fold_in(stream_key, 6), dim), (parts,), jnp.float32, smallest / len(pieces), top_value / len(pieces))
        return jnp.repeat(jnp.exp(heights), dims[dim] // parts).reshape((-1,) + (1,) * (len(dims) - dim - 1))

    level = one(*pieces[0])
    for cut in pieces[1:]:
        level = level * one(*cut)
    return level


def centred(key, extent, width, most, cuts=(), held_as=jnp.bfloat16):
    factor_of = block_scale(key, extent, cuts, -0.22, 0.18) if cuts else 1.0
    result = jax.random.normal(key, extent, jnp.float32) * width * factor_of
    return jnp.minimum(jnp.maximum(result, -most), most).astype(held_as)


def setup_inputs(seed: int = 0) -> dict:
    key_of = jax.random.split(jax.random.key(seed), 8)
    tokens = centred(key_of[0], (P_SIZE, F, D), 1.0, 6.0, ((0, 4), (1, 8)))
    norm_gain = jnp.clip(1.0 + 0.15 * jax.random.normal(key_of[1], (D,), jnp.float32), 0.25, 1.75)
    qk_gain = draw_qk_gain(jax.random.fold_in(key_of[7], 71), 0)
    window_blocks = draw_window_blocks(jax.random.fold_in(key_of[7], 71), 0)
    w_spatial = draw_w_spatial(jax.random.fold_in(key_of[7], 71), 0)
    w_temporal = draw_w_temporal(jax.random.fold_in(key_of[7], 71), 0)
    w_out = centred(key_of[6], (D, 2, HEADS * HD), (2 * HEADS * HD) ** -0.5, 0.09375, ((0, 8), (2, 4)))
    return {"tokens": tokens, "norm_gain": norm_gain, "qk_gain": qk_gain, "window_blocks": window_blocks, "w_spatial": w_spatial, "w_temporal": w_temporal, "w_out": w_out}


def rms_scale(values):
    return values * lax.rsqrt(lax.optimization_barrier(jnp.mean(values * values, axis=-1, keepdims=True)) + 1e-06)

def finish_heads(projected, gain_pair, head_count):
    head_width = gain_pair.shape[-1]
    shaped = projected.reshape(projected.shape[0], projected.shape[1], 3, head_count, head_width)
    queries = (rms_scale(shaped[:, :, 0]) * gain_pair[0] * head_width ** (-0.5)).astype(jnp.bfloat16)
    key_rows = (rms_scale(shaped[:, :, 1]) * gain_pair[1]).astype(jnp.bfloat16)
    values = shaped[:, :, 2].astype(jnp.bfloat16)
    return (queries, key_rows, values)

def spatial_attention(queries, key_rows, values, window_blocks, tile_rows):
    row_total, frames, head_count, head_width = queries.shape
    tile_count = row_total // tile_rows
    listed = window_blocks.shape[1]
    query_tiles = queries.reshape(tile_count, tile_rows, frames, head_count, head_width).astype(jnp.float32)
    key_tiles = key_rows.reshape(tile_count, tile_rows, frames, head_count, head_width)[window_blocks]
    key_tiles = key_tiles.reshape(tile_count, listed * tile_rows, frames, head_count, head_width).astype(jnp.float32)
    value_tiles = values.reshape(tile_count, tile_rows, frames, head_count, head_width)[window_blocks]
    value_tiles = value_tiles.reshape(tile_count, listed * tile_rows, frames, head_count, head_width).astype(jnp.float32)
    scores = jnp.einsum('tqfhe,tkfhe->tfhqk', query_tiles, key_tiles)
    scores = jnp.exp(scores - lax.optimization_barrier(jnp.max(scores, axis=-1, keepdims=True)))
    attn_weights = (scores / lax.optimization_barrier(jnp.sum(scores, axis=-1, keepdims=True))).astype(jnp.bfloat16)
    attended = jnp.einsum('tfhqk,tkfhe->tqfhe', attn_weights.astype(jnp.float32), value_tiles)
    return attended.astype(jnp.bfloat16).reshape(row_total, frames, head_count, head_width)

def temporal_attention(queries, key_rows, values):
    frames = queries.shape[1]
    scores = jnp.einsum('rfhe,rghe->rhfg', queries.astype(jnp.float32), key_rows.astype(jnp.float32))
    causal = lax.broadcasted_iota(jnp.int32, (frames, frames), 1) <= lax.broadcasted_iota(jnp.int32, (frames, frames), 0)
    scores = jnp.where(causal, scores, jnp.float32(-1e+30))
    scores = jnp.exp(scores - lax.optimization_barrier(jnp.max(scores, axis=-1, keepdims=True)))
    attn_weights = (scores / lax.optimization_barrier(jnp.sum(scores, axis=-1, keepdims=True))).astype(jnp.bfloat16)
    attended = jnp.einsum('rhfg,rghe->rfhe', attn_weights.astype(jnp.float32), values.astype(jnp.float32))
    return attended.astype(jnp.bfloat16)

def reference(tokens, norm_gain, qk_gain, window_blocks, w_spatial, w_temporal, w_out):
    normed = (rms_scale(tokens.astype(jnp.float32)) * norm_gain).astype(jnp.bfloat16)
    flattened = normed.reshape(P_SIZE * F, D)
    spatial_proj = jnp.dot(flattened, w_spatial.reshape(D, 3 * HEADS * HD), preferred_element_type=jnp.float32)
    spatial_q, spatial_k, spatial_v = finish_heads(spatial_proj.reshape(P_SIZE, F, 3 * HEADS * HD), qk_gain[0], HEADS)
    spatial_out = spatial_attention(spatial_q, spatial_k, spatial_v, window_blocks, TILE)
    temporal_proj = jnp.dot(flattened, w_temporal.reshape(D, 3 * HEADS * HD), preferred_element_type=jnp.float32)
    temporal_q, temporal_k, temporal_v = finish_heads(temporal_proj.reshape(P_SIZE, F, 3 * HEADS * HD), qk_gain[1], HEADS)
    temporal_out = temporal_attention(temporal_q, temporal_k, temporal_v)
    branch_out = jnp.stack([spatial_out, temporal_out], axis=2).reshape(P_SIZE, F, 2, N_GRP, HEADS_DEV * HD)
    grouped = w_out.reshape(D, 2, N_GRP, HEADS_DEV * HD)
    summed = jnp.zeros((P_SIZE, F, D), jnp.float32)
    for head_group in range(N_GRP):
        partial_sum = jnp.einsum('pfbc,dbc->pfd', branch_out[:, :, :, head_group].astype(jnp.float32), grouped[:, :, head_group].astype(jnp.float32))
        rounded = lax.optimization_barrier(partial_sum.astype(jnp.bfloat16))
        summed = summed + rounded.astype(jnp.float32)
    return (tokens.astype(jnp.float32) + summed).astype(jnp.bfloat16)
```

```python
import jax
import jax.numpy as jnp
from jax import lax
from jax.experimental import pallas as pl
from jax.experimental.pallas import tpu as pltpu
from jax.sharding import PartitionSpec as P

TILE = 128
EPS = 1e-06
VMEM_BYTES = 32 * 1024 * 1024
VMEM = pl.BlockSpec(memory_space=pltpu.VMEM)


def params():
    return pltpu.CompilerParams(vmem_limit_bytes=VMEM_BYTES)


def estimate(flops, *arrays):
    size = sum(a.size * a.dtype.itemsize for a in arrays)
    return pl.CostEstimate(flops=int(flops), bytes_accessed=int(size), transcendentals=0)


def project(rows, weights, gains, seq_split):
    frames = len(rows)
    row_count, depth = rows[0].shape
    split, _, _, columns = weights.shape
    heads, width = gains.shape[1], gains.shape[3]
    part = row_count // split

    def kernel(*refs):
        row_refs, w_ref, gain_ref, out_refs = refs[:frames], refs[frames], refs[frames + 1], refs[frames + 2 :]
        kind = pl.program_id(0)
        w = w_ref[...].reshape(depth, columns)
        for f in range(frames):
            projected = jnp.dot(row_refs[f][...], w, preferred_element_type=jnp.float32)

            def store(h, values):
                at = pl.ds(h * width, width)
                if seq_split:
                    out_refs[0][:, f, :, at] = values.reshape(split, part, width).astype(jnp.bfloat16)
                else:
                    out_refs[f][:, at] = values.astype(jnp.bfloat16)

            @pl.when(kind < 2)
            def _():
                for h in range(heads):
                    one = projected[:, h * width : (h + 1) * width]
                    scale = lax.rsqrt(jnp.mean(one * one, axis=-1, keepdims=True) + EPS)
                    store(h, one * scale * gain_ref[0, h])

            @pl.when(kind == 2)
            def _():
                for h in range(heads):
                    store(h, projected[:, h * width : (h + 1) * width])

    if seq_split:
        out_shape = [jax.ShapeDtypeStruct((split, frames, part, 3 * columns), jnp.bfloat16)]
        out_specs = [pl.BlockSpec((split, frames, part, columns), lambda j: (0, 0, 0, j))]
    else:
        out_shape = [jax.ShapeDtypeStruct((row_count, 3 * columns), jnp.bfloat16)] * frames
        out_specs = [pl.BlockSpec((row_count, columns), lambda j: (0, j))] * frames
    return pl.pallas_call(
        kernel,
        grid=(3,),
        in_specs=[pl.BlockSpec((row_count, depth), lambda j: (0, 0))] * frames
        + [
            pl.BlockSpec((split, None, depth // split, columns), lambda j: (0, j, 0, 0)),
            pl.BlockSpec((1, heads, 1, width), lambda j: (j, 0, 0, 0)),
        ],
        out_specs=out_specs,
        out_shape=out_shape,
        compiler_params=params(),
        cost_estimate=estimate(
            2 * frames * row_count * depth * 3 * columns, *rows, weights, *out_shape
        ),
        name="project_temporal" if seq_split else "project_spatial",
    )(*rows, weights, gains)


def temporal_attention(packed, heads):
    split, frames_each, patches, columns = packed.shape
    frames = split * frames_each
    width = columns // (3 * heads)
    group = min(patches, max(256 // frames, 8))
    unit = frames * group

    def kernel(x_ref, out_ref):
        row = lax.broadcasted_iota(jnp.int32, (unit, unit), 0)
        col = lax.broadcasted_iota(jnp.int32, (unit, unit), 1)
        seen = (row % group == col % group) & (col // group <= row // group)

        def read(first, kind, h):
            at = (kind * heads + h) * width
            piece = x_ref[:, :, first : first + group, at : at + width]
            if group % 16:
                return piece.astype(jnp.float32).reshape(unit, width).astype(jnp.bfloat16)
            return piece.reshape(unit, width)

        for first in range(0, patches, group):
            for h in range(heads):
                q, k, v = (read(first, kind, h) for kind in range(3))
                scores = lax.dot_general(
                    q, k, (((1,), (1,)), ((), ())), preferred_element_type=jnp.float32
                )
                scores = jnp.where(seen, scores, jnp.float32(-1e30))
                scores = jnp.exp(scores - jnp.max(scores, axis=-1, keepdims=True))
                total = jnp.sum(scores, axis=-1, keepdims=True)
                attended = jnp.dot(
                    scores.astype(jnp.bfloat16), v, preferred_element_type=jnp.float32
                )
                attended = (attended / total).reshape(split, frames_each, group, width)
                out_ref[:, :, first : first + group, h * width : (h + 1) * width] = (
                    attended.astype(jnp.bfloat16)
                )

    out_shape = jax.ShapeDtypeStruct((split, frames_each, patches, heads * width), jnp.bfloat16)
    return pl.pallas_call(
        kernel,
        in_specs=[VMEM],
        out_specs=VMEM,
        out_shape=out_shape,
        compiler_params=params(),
        cost_estimate=estimate(
            4 * unit * unit * width * heads * (patches // group), packed, out_shape
        ),
        name="temporal_attention",
    )(packed)


def finish_block(slot, frame, slots, temporal_out, w_out, table, arrived, heads):
    count = len(slots)
    row_count, columns = slots[0].shape
    columns //= 3
    width = columns // heads
    tiles_each = row_count // TILE
    listed = table.shape[1]
    split, _, _, depth = w_out.shape
    part = temporal_out.shape[2]

    def kernel(*refs):
        table_ref, slot_refs = refs[0], refs[1 : 1 + count]
        t_ref, w_ref = refs[1 + count], refs[2 + count]
        arrived_ref = refs[3 + count] if arrived is not None else None
        out_ref, k_ref, v_ref, o_ref = refs[-4:]
        for s in range(count):
            for i in range(tiles_each):
                at = pl.ds(i * TILE, TILE)
                k_ref[s * tiles_each + i] = slot_refs[s][at, columns : 2 * columns]
                v_ref[s * tiles_each + i] = slot_refs[s][at, 2 * columns :]
        for i in range(tiles_each):
            picks = [table_ref[slot * tiles_each + i, j] for j in range(listed)]
            for h in range(heads):
                at = pl.ds(h * width, width)
                q = slot_refs[slot][pl.ds(i * TILE, TILE), at]
                k = jnp.concatenate([k_ref[p, :, at] for p in picks], axis=0)
                v = jnp.concatenate([v_ref[p, :, at] for p in picks], axis=0)
                scores = lax.dot_general(
                    q, k, (((1,), (1,)), ((), ())), preferred_element_type=jnp.float32
                )
                scores = jnp.exp(scores - jnp.max(scores, axis=-1, keepdims=True))
                total = jnp.sum(scores, axis=-1, keepdims=True)
                attended = jnp.dot(
                    scores.astype(jnp.bfloat16), v, preferred_element_type=jnp.float32
                )
                o_ref[pl.ds(i * TILE, TILE), at] = (attended / total).astype(jnp.bfloat16)
        spatial = o_ref[...]
        if part % 16:
            temporal = (
                t_ref[:, frame].astype(jnp.float32).reshape(row_count, columns).astype(jnp.bfloat16)
            )
        else:
            temporal = t_ref[:, frame].reshape(row_count, columns)
        for s in range(split):
            at = pl.ds(s * depth, depth)
            value = jnp.dot(spatial, w_ref[s, 0], preferred_element_type=jnp.float32)
            value += jnp.dot(temporal, w_ref[s, 1], preferred_element_type=jnp.float32)
            if arrived_ref is not None:
                value += arrived_ref[:, at].astype(jnp.float32)
            out_ref[:, at] = value.astype(jnp.bfloat16)

    out_shape = jax.ShapeDtypeStruct((row_count, split * depth), jnp.bfloat16)
    operands = [table, *slots, temporal_out, w_out] + ([] if arrived is None else [arrived])
    flops = 4 * row_count * listed * TILE * columns + 4 * row_count * columns * split * depth
    return pl.pallas_call(
        kernel,
        in_specs=[pl.BlockSpec(memory_space=pltpu.SMEM)] + [VMEM] * (len(operands) - 1),
        out_specs=VMEM,
        out_shape=out_shape,
        scratch_shapes=[
            pltpu.VMEM((count * tiles_each, TILE, columns), jnp.bfloat16),
            pltpu.VMEM((count * tiles_each, TILE, columns), jnp.bfloat16),
            pltpu.VMEM((row_count, columns), jnp.bfloat16),
        ],
        compiler_params=params(),
        cost_estimate=estimate(flops, *operands, out_shape),
        name="finish_block",
    )(*operands)


def slot_order(window_blocks, me, ring, tiles_each):
    def renumber(tile):
        return (me - tile // tiles_each + ring) % ring * tiles_each + tile % tiles_each

    rows = renumber(jnp.arange(ring * tiles_each, dtype=jnp.int32))
    return renumber(window_blocks[rows])


def body(tokens, norm_gain, qk_gain, window_blocks, w_spatial, w_temporal, w_out):
    rows_here, frames_here, _ = tokens.shape
    heads, width = qk_gain.shape[2:]
    ring = lax.axis_size("grp")
    me = lax.axis_index("grp")
    forward = [(i, (i + 1) % ring) for i in range(ring)]

    full_temporal = lax.all_gather(w_temporal.transpose(1, 0, 2), "seq", axis=0)
    full_spatial = lax.all_gather(w_spatial.transpose(1, 0, 2), "seq", axis=0)
    full_out = lax.all_gather(w_out.transpose(1, 2, 0), "seq", axis=0)

    wide = tokens.astype(jnp.float32)
    normed = (
        wide * lax.rsqrt(jnp.mean(wide * wide, axis=-1, keepdims=True) + EPS) * norm_gain
    ).astype(jnp.bfloat16)
    held = [normed[:, f] for f in range(frames_here)]

    gains = jnp.concatenate([qk_gain, jnp.ones_like(qk_gain[:, :1])], axis=1)
    gains = gains * jnp.array([width**-0.5, 1.0, 1.0], jnp.float32)[None, :, None, None]
    gains = gains[:, :, :, None, :]
    table = slot_order(window_blocks, me, ring, rows_here // TILE)

    temporal_outs, slots = [], []
    for step in range(ring):
        last = step == ring - 1
        coming = None if last else [lax.ppermute(x, "grp", forward) for x in held]
        packed = project(held, full_temporal, gains[1], True)[0]
        exchanged = lax.all_to_all(packed, "seq", split_axis=0, concat_axis=0, tiled=True)
        attended = temporal_attention(exchanged, heads)
        temporal_outs.append(
            lax.all_to_all(attended, "seq", split_axis=0, concat_axis=0, tiled=True)
        )
        if last:
            slots.append([project([x], full_spatial, gains[0], False)[0] for x in held])
        else:
            slots.append(project(held, full_spatial, gains[0], False))
        held = coming

    def finish(slot, frame, arrived):
        return finish_block(
            slot, frame, [s[frame] for s in slots], temporal_outs[slot], full_out, table, arrived, heads
        )

    sums = [None] * frames_here
    for slot in range(1, ring):
        for f in range(frames_here):
            sums[f] = lax.ppermute(finish(slot, f, sums[f]), "grp", forward)
    own = [finish(0, f, None) for f in range(frames_here)]
    total = jnp.stack(
        [o.astype(jnp.float32) + s.astype(jnp.float32) for o, s in zip(own, sums)], axis=1
    )
    return (wide + total).astype(jnp.bfloat16)


def solution(mesh):
    return jax.shard_map(
        body,
        mesh=mesh,
        in_specs=(
            P("grp", "seq", None),
            P(),
            P(None, None, "grp", None),
            P(),
            P("seq", None, "grp"),
            P("seq", None, "grp"),
            P("seq", None, "grp"),
        ),
        out_specs=P("grp", "seq", None),
        check_vma=False,
    )
```

```python
import itertools

import jax
import jax.numpy as jnp
from jax import lax
from jax.experimental import pallas as pl
from jax.experimental.pallas import tpu as pltpu
from jax.sharding import PartitionSpec as P

TILE = 128
PROJECT_WEIGHT, LIGHT_WEIGHT = 3, 10
EPS = 1e-06
VMEM_BYTES = 56 * 1024 * 1024
VMEM = pl.BlockSpec(memory_space=pltpu.VMEM)
ANY = pl.BlockSpec(memory_space=pl.ANY)
MARK = jax.ShapeDtypeStruct((8, 128), jnp.float32)


def params():
    return pltpu.CompilerParams(vmem_limit_bytes=VMEM_BYTES)


def dot_transposed(a, b):
    return lax.dot_general(a, b, (((1,), (1,)), ((), ())), preferred_element_type=jnp.float32)


class Order:
    def __init__(self):
        self.mark = None

    def call(self, kernel, operands, in_specs, out_specs, out_shape, flops, ordered=False, **more):
        count = len(operands)
        marked = ordered and self.mark is not None

        def run(*refs):
            rest = refs[count + marked :]
            kernel(*refs[:count], *rest[: len(out_shape)], *rest[len(out_shape) + ordered :])

        outs = pl.pallas_call(
            run,
            in_specs=in_specs + [ANY] * marked,
            out_specs=out_specs + [ANY] * ordered,
            out_shape=out_shape + [MARK] * ordered,
            compiler_params=params(),
            cost_estimate=pl.CostEstimate(flops=flops, bytes_accessed=0, transcendentals=0),
            **more,
        )(*operands, *([self.mark] * marked))
        if ordered:
            *outs, self.mark = outs
        return outs


def relay(order, arrays):
    return order.call(
        lambda *refs: None,
        arrays,
        [ANY] * len(arrays),
        [ANY] * len(arrays),
        [jax.ShapeDtypeStruct(x.shape, x.dtype) for x in arrays],
        0,
        ordered=True,
        input_output_aliases={i: i for i in range(len(arrays))},
        name="relay",
    )


SPATIAL, TEMPORAL = 0, 1


def project(order, tasks, weights, gains):
    arrays = []
    for _, groups in tasks:
        arrays += [x for group in groups for x in group if not any(x is y for y in arrays)]
    row_count, depth = arrays[0].shape
    split, _, _, columns = weights.shape
    heads, width = gains.shape[2], gains.shape[4]
    part = row_count // split
    together = max(1, min(heads, 256 // width))
    span = together * width

    def index(x):
        return [y is x for y in arrays].index(True)

    def branch_at(j):
        found = tasks[0][0]
        for t in range(1, len(tasks)):
            found = jnp.where(j >= 3 * t, tasks[t][0], found)
        return found

    out_shape, out_specs, writes = [], [], []
    for t, (branch, groups) in enumerate(tasks):

        def place(j, t=t):
            return jnp.clip(j - 3 * t, 0, 2)

        writes.append([])
        for g, group in enumerate(groups):
            frames = len(group)
            for f, x in enumerate(group):
                first = len(out_shape) + (f if branch == SPATIAL else 0)
                writes[-1].append((index(x), first, g, f))
            if branch == SPATIAL:
                out_shape += [jax.ShapeDtypeStruct((row_count, 3 * columns), jnp.bfloat16)] * frames
                out_specs += [
                    pl.BlockSpec((row_count, columns), lambda j, place=place: (0, place(j)))
                ] * frames
        if branch == TEMPORAL:
            whole = (split, len(groups), len(groups[0]), part, 3 * columns)
            out_shape.append(jax.ShapeDtypeStruct(whole, jnp.bfloat16))
            out_specs.append(
                pl.BlockSpec(
                    whole[:-1] + (columns,), lambda j, place=place: (0, 0, 0, 0, place(j))
                )
            )

    def kernel(*refs):
        row_refs, w_ref, gain_ref = refs[: len(arrays)], refs[len(arrays)], refs[len(arrays) + 1]
        out_refs = refs[len(arrays) + 2 :]
        step = pl.program_id(0)
        kind = step % 3

        def run(t):
            for start in range(0, heads, together):
                w = w_ref[:, :, start * width : start * width + span].reshape(depth, span)
                for source, target, g, f in writes[t]:
                    projected = jnp.dot(
                        row_refs[source][...], w, preferred_element_type=jnp.float32
                    )
                    for h in range(together):
                        one = projected[:, h * width : (h + 1) * width]
                        scale = lax.rsqrt(jnp.mean(one * one, axis=-1, keepdims=True) + EPS)
                        scale = jnp.where(kind < 2, scale, 1.0)
                        one = one * scale * gain_ref[start + h]
                        at = pl.ds((start + h) * width, width)
                        if tasks[t][0] == TEMPORAL:
                            out_refs[target][:, g, f, :, at] = one.reshape(split, part, width).astype(
                                jnp.bfloat16
                            )
                        else:
                            out_refs[target][:, at] = one.astype(jnp.bfloat16)

        for t in range(len(tasks)):
            if len(tasks) == 1:
                run(t)
            else:
                pl.when(step // 3 == t)(lambda t=t: run(t))

    outs = order.call(
        kernel,
        [*arrays, weights, gains],
        [pl.BlockSpec((row_count, depth), lambda j: (0, 0), pipeline_mode=pl.Buffered(1))]
        * len(arrays)
        + [
            pl.BlockSpec(
                (split, None, depth // split, columns),
                lambda j: (0, 3 * branch_at(j) + j % 3, 0, 0),
            ),
            pl.BlockSpec((None, None, heads, 1, width), lambda j: (branch_at(j), j % 3, 0, 0, 0)),
        ],
        out_specs,
        out_shape,
        6 * sum(map(len, writes)) * row_count * depth * columns * PROJECT_WEIGHT,
        ordered=True,
        grid=(3 * len(tasks),),
        name="project",
    )
    outs, found = list(outs), []
    for branch, groups in tasks:
        if branch == TEMPORAL:
            found.append(outs.pop(0))
        else:
            found.append([[outs.pop(0) for _ in group] for group in groups])
    return found


def temporal_attention(order, packed, heads, ordered):
    split, chunks, frames_each, patches, columns = packed.shape
    frames = split * frames_each
    width = columns // (3 * heads)
    group = min(patches, max(256 // frames, 8))
    unit = frames * group

    def kernel(x_ref, out_ref):
        row = lax.broadcasted_iota(jnp.int32, (unit, unit), 0)
        col = lax.broadcasted_iota(jnp.int32, (unit, unit), 1)
        seen = (row % group == col % group) & (col // group <= row // group)

        def read(c, first, kind, h):
            at = (kind * heads + h) * width
            piece = x_ref[:, c, :, first : first + group, at : at + width]
            if group % 16:
                return piece.astype(jnp.float32).reshape(unit, width).astype(jnp.bfloat16)
            return piece.reshape(unit, width)

        for c, first in itertools.product(range(chunks), range(0, patches, group)):
            for h in range(heads):
                q, k, v = (read(c, first, kind, h) for kind in range(3))
                scores = dot_transposed(q, k)
                scores = jnp.where(seen, scores, jnp.float32(-1e30))
                scores = jnp.exp(scores - jnp.max(scores, axis=-1, keepdims=True))
                total = jnp.sum(scores, axis=-1, keepdims=True)
                attended = jnp.dot(
                    scores.astype(jnp.bfloat16), v, preferred_element_type=jnp.float32
                )
                attended = (attended / total).reshape(split, frames_each, group, width)
                out_ref[:, c, :, first : first + group, h * width : (h + 1) * width] = (
                    attended.astype(jnp.bfloat16)
                )

    return order.call(
        kernel,
        [packed],
        [VMEM],
        [VMEM],
        [jax.ShapeDtypeStruct(packed.shape[:-1] + (heads * width,), jnp.bfloat16)],
        4 * unit * unit * width * heads * chunks * (patches // group) // LIGHT_WEIGHT,
        ordered=ordered,
        name="temporal_attention",
    )[0]


def finish_block(order, slot, frame, slots, temporal_out, w_out, table, arrived, heads, ordered):
    count = len(slots)
    row_count, columns = slots[0].shape
    columns //= 3
    width = columns // heads
    tiles_each = row_count // TILE
    listed = table.shape[1]
    split, _, depth, _ = w_out.shape
    part = temporal_out.shape[3]
    adds = arrived is not None

    def kernel(*refs):
        table_ref, slot_refs = refs[0], refs[1 : 1 + count]
        t_hbm, w_hbm = refs[1 + count], refs[2 + count]
        out_ref, q_ref, k_ref, v_ref, t_ref, w_ref, o_ref, sems = refs[3 + count + adds :][:8]

        copies = []

        def copy(source, target):
            copies.append(pltpu.make_async_copy(source, target, sems.at[len(copies)]))
            copies[-1].start()
            return copies[-1]

        first = [copy(slot_refs[slot].at[:, pl.ds(0, columns)], q_ref)]
        for s in range(count):
            at = pl.ds(s * row_count, row_count)
            first.append(copy(slot_refs[s].at[:, pl.ds(columns, columns)], k_ref.at[at]))
            first.append(copy(slot_refs[s].at[:, pl.ds(2 * columns, columns)], v_ref.at[at]))
        second = [copy(t_hbm.at[:, 0, frame], t_ref), copy(w_hbm, w_ref)]
        if adds:
            arrived_ref = refs[-1]
            second.append(copy(refs[3 + count], arrived_ref))
        for one in first:
            one.wait()
        for i in range(tiles_each):
            picks = [
                pl.ds(pl.multiple_of(table_ref[slot * tiles_each + i, j] * TILE, TILE), TILE)
                for j in range(listed)
            ]
            for h in range(heads):
                at = pl.ds(h * width, width)
                q = q_ref[pl.ds(i * TILE, TILE), at]
                k = jnp.concatenate([k_ref[p, at] for p in picks], axis=0)
                v = jnp.concatenate([v_ref[p, at] for p in picks], axis=0)
                scores = dot_transposed(q, k)
                scores = jnp.exp(scores - jnp.max(scores, axis=-1, keepdims=True))
                total = jnp.sum(scores, axis=-1, keepdims=True)
                attended = jnp.dot(
                    scores.astype(jnp.bfloat16), v, preferred_element_type=jnp.float32
                )
                o_ref[pl.ds(i * TILE, TILE), at] = (attended / total).astype(jnp.bfloat16)
        for one in second:
            one.wait()
        spatial = o_ref[...]
        temporal = t_ref[...]
        if part % 16:
            temporal = temporal.astype(jnp.float32)
        temporal = temporal.reshape(row_count, columns).astype(jnp.bfloat16)
        for s in range(split):
            at = pl.ds(s * depth, depth)
            value = dot_transposed(spatial, w_ref[s, 0]) + dot_transposed(temporal, w_ref[s, 1])
            if adds:
                value += arrived_ref[:, at].astype(jnp.float32)
            out_ref[:, at] = value.astype(jnp.bfloat16)

    operands = [table, *slots, temporal_out, w_out] + [arrived] * adds
    held = (row_count, split * depth)
    scratch = [
        pltpu.VMEM((row_count, columns), jnp.bfloat16),
        pltpu.VMEM((count * row_count, columns), jnp.bfloat16),
        pltpu.VMEM((count * row_count, columns), jnp.bfloat16),
        pltpu.VMEM((split, part, columns), jnp.bfloat16),
        pltpu.VMEM((split, 2, depth, columns), jnp.bfloat16),
        pltpu.VMEM((row_count, columns), jnp.bfloat16),
        pltpu.SemaphoreType.DMA((2 * count + 4,)),
    ]
    return order.call(
        kernel,
        operands,
        [pl.BlockSpec(memory_space=pltpu.SMEM)] + [ANY] * (len(operands) - 1),
        [VMEM],
        [jax.ShapeDtypeStruct(held, jnp.bfloat16)],
        (4 * row_count * listed * TILE * columns + 4 * row_count * columns * split * depth)
        // LIGHT_WEIGHT,
        ordered=ordered,
        scratch_shapes=scratch + [pltpu.VMEM(held, jnp.bfloat16)] * adds,
        name="finish_block",
    )[0]


def slot_order(window_blocks, me, ring, tiles_each):
    def renumber(tile):
        return (me - tile // tiles_each + ring) % ring * tiles_each + tile % tiles_each

    rows = renumber(jnp.arange(ring * tiles_each, dtype=jnp.int32))
    return renumber(window_blocks[rows])


def body(tokens, norm_gain, qk_gain, window_blocks, w_spatial, w_temporal, w_out):
    rows_here, frames_here, _ = tokens.shape
    heads, width = qk_gain.shape[2:]
    ring = lax.axis_size("grp")
    me = lax.axis_index("grp")
    forward = [(i, (i + 1) % ring) for i in range(ring)]
    order = Order()

    def send(arrays):
        return [lax.ppermute(x, "grp", forward) for x in arrays]

    def swap(array):
        return lax.all_to_all(array, "seq", split_axis=0, concat_axis=0, tiled=True)

    wide = tokens.astype(jnp.float32)
    normed = (
        wide * lax.rsqrt(jnp.mean(wide * wide, axis=-1, keepdims=True) + EPS) * norm_gain
    ).astype(jnp.bfloat16)
    full_qkv = lax.all_gather(
        jnp.concatenate([w_spatial.transpose(1, 0, 2), w_temporal.transpose(1, 0, 2)]),
        "seq",
        axis=0,
    )
    full_out = lax.all_gather(w_out.transpose(1, 0, 2), "seq", axis=0)
    gains = jnp.concatenate([qk_gain, jnp.ones_like(qk_gain[:, :1])], axis=1)
    gains = gains * jnp.array([width**-0.5, 1.0, 1.0], jnp.float32)[None, :, None, None]
    gains = gains[:, :, :, None, :]
    table = slot_order(window_blocks, me, ring, rows_here // TILE)

    def temporal(k):
        (packed,) = project(order, [(TEMPORAL, [chunks[k]])], full_qkv, gains)
        exchanged[k] = swap(packed)

    def attend(k, ordered=False):
        temporal_outs[k] = swap(temporal_attention(order, exchanged[k], heads, ordered))

    def spatial(ks):
        tasks = [(SPATIAL, [chunks[k] for k in ks])]
        slots.update(zip(ks, project(order, tasks, full_qkv, gains)[0]))

    def finish(slot, frame, arrived, ordered=False):
        return finish_block(
            order,
            slot,
            frame,
            [slots[k][frame] for k in range(ring)],
            temporal_outs[slot],
            full_out,
            table,
            arrived,
            heads,
            ordered,
        )

    last = ring - 1
    chunks = [[normed[:, f] for f in range(frames_here)]]
    chunks += [[None] * frames_here for _ in range(last)]
    slots, exchanged, temporal_outs, arrived, sums = {}, {}, {}, {}, []
    for window in range(last + frames_here - 1):
        if arrived:
            for (k, f), x in zip(arrived, relay(order, list(arrived.values()))):
                chunks[k][f] = x
        steps = [window + 1 - f for f in range(frames_here)]
        moving = [(k, f) for f, k in enumerate(steps) if 1 <= k <= last]
        arrived = {(k, f): send([chunks[k - 1][f]])[0] for k, f in moving}
        ready = window - frames_here + 1
        if ready == 1 and last > 1:
            temporal(1)
            spatial([1, 0])
            temporal(0)
        elif ready > 0:
            at_end = ready == last - 1
            if at_end:
                attend(1, True)
            some = chunks[last][:-1] if at_end and frames_here > 1 else []
            tasks = [
                (SPATIAL, [chunks[ready]] + ([some] if some else [])),
                (TEMPORAL, [chunks[ready]]),
            ]
            found = project(order, tasks, full_qkv, gains)
            slots[ready], exchanged[ready] = found[0][0], swap(found[1])
            if some:
                slots[last] = found[0][1]
                sums = [finish(1, f, None, True) for f in range(len(some))]
    for (k, f), x in arrived.items():
        chunks[k][f] = x
    if last == 1:
        temporal(1)
        spatial([0])
        temporal(0)
        attend(1, True)
    have = slots.setdefault(last, [])
    tasks = [(SPATIAL, [chunks[last][len(have) :]])]
    have += project(order, tasks, full_qkv, gains)[0][0]
    sums = send(sums + [finish(1, f, None) for f in range(len(sums), frames_here)])
    if last > 1:
        temporal(last)
    for k in range(ring):
        if k not in temporal_outs:
            attend(k)
    for slot in range(2, ring):
        sums = send([finish(slot, f, sums[f]) for f in range(frames_here)])
    own = [finish(0, f, None) for f in range(frames_here)]
    total = jnp.stack(
        [o.astype(jnp.float32) + s.astype(jnp.float32) for o, s in zip(own, sums)], axis=1
    )
    return (wide + total).astype(jnp.bfloat16)


def solution(mesh):
    return jax.shard_map(
        body,
        mesh=mesh,
        in_specs=(
            P("grp", "seq", None),
            P(),
            P(None, None, "grp", None),
            P(),
            P("seq", None, "grp"),
            P("seq", None, "grp"),
            P("seq", None, "grp"),
        ),
        out_specs=P("grp", "seq", None),
        check_vma=False,
    )
```

```python
import itertools

import jax
import jax.numpy as jnp
from jax import lax
from jax.experimental import pallas as pl
from jax.experimental.pallas import tpu as pltpu
from jax.sharding import PartitionSpec as P

TILE = 128
PROJECT_WEIGHT, LIGHT_WEIGHT = 3, 10
EPS = 1e-06
VMEM_BYTES = 56 * 1024 * 1024
VMEM = pl.BlockSpec(memory_space=pltpu.VMEM)
ANY = pl.BlockSpec(memory_space=pl.ANY)
MARK = jax.ShapeDtypeStruct((8, 128), jnp.float32)


def params():
    return pltpu.CompilerParams(vmem_limit_bytes=VMEM_BYTES)


def dot_transposed(a, b):
    return lax.dot_general(a, b, (((1,), (1,)), ((), ())), preferred_element_type=jnp.float32)


class Order:
    def __init__(self):
        self.mark = None

    def call(self, kernel, operands, in_specs, out_specs, out_shape, flops, ordered=False, **more):
        count = len(operands)
        marked = ordered and self.mark is not None

        def run(*refs):
            rest = refs[count + marked :]
            kernel(*refs[:count], *rest[: len(out_shape)], *rest[len(out_shape) + ordered :])

        outs = pl.pallas_call(
            run,
            in_specs=in_specs + [ANY] * marked,
            out_specs=out_specs + [ANY] * ordered,
            out_shape=out_shape + [MARK] * ordered,
            compiler_params=params(),
            cost_estimate=pl.CostEstimate(flops=flops, bytes_accessed=0, transcendentals=0),
            **more,
        )(*operands, *([self.mark] * marked))
        if ordered:
            *outs, self.mark = outs
        return outs


def relay(order, arrays):
    return order.call(
        lambda *refs: None,
        arrays,
        [ANY] * len(arrays),
        [ANY] * len(arrays),
        [jax.ShapeDtypeStruct(x.shape, x.dtype) for x in arrays],
        0,
        ordered=True,
        input_output_aliases={i: i for i in range(len(arrays))},
        name="relay",
    )


SPATIAL, TEMPORAL = 0, 1


def project(order, tasks, weights, gains):
    arrays = []
    for _, groups in tasks:
        arrays += [x for group in groups for x in group if not any(x is y for y in arrays)]
    row_count, depth = arrays[0].shape
    split, _, _, columns = weights.shape
    heads, width = gains.shape[2], gains.shape[4]
    part = row_count // split
    together = max(1, min(heads, 256 // width))
    span = together * width

    def index(x):
        return [y is x for y in arrays].index(True)

    def branch_at(j):
        found = tasks[0][0]
        for t in range(1, len(tasks)):
            found = jnp.where(j >= 3 * t, tasks[t][0], found)
        return found

    out_shape, out_specs, writes = [], [], []
    for t, (branch, groups) in enumerate(tasks):

        def place(j, t=t):
            return jnp.clip(j - 3 * t, 0, 2)

        writes.append([])
        for g, group in enumerate(groups):
            frames = len(group)
            for f, x in enumerate(group):
                first = len(out_shape) + (f if branch == SPATIAL else 0)
                writes[-1].append((index(x), first, g, f))
            if branch == SPATIAL:
                out_shape += [jax.ShapeDtypeStruct((row_count, 3 * columns), jnp.bfloat16)] * frames
                out_specs += [
                    pl.BlockSpec((row_count, columns), lambda j, place=place: (0, place(j)))
                ] * frames
        if branch == TEMPORAL:
            whole = (split, len(groups), len(groups[0]), part, 3 * columns)
            out_shape.append(jax.ShapeDtypeStruct(whole, jnp.bfloat16))
            out_specs.append(
                pl.BlockSpec(
                    whole[:-1] + (columns,), lambda j, place=place: (0, 0, 0, 0, place(j))
                )
            )

    def kernel(*refs):
        row_refs, w_ref, gain_ref = refs[: len(arrays)], refs[len(arrays)], refs[len(arrays) + 1]
        out_refs = refs[len(arrays) + 2 :]
        step = pl.program_id(0)
        kind = step % 3

        def run(t):
            for start in range(0, heads, together):
                w = w_ref[:, :, start * width : start * width + span].reshape(depth, span)
                for source, target, g, f in writes[t]:
                    projected = jnp.dot(
                        row_refs[source][...], w, preferred_element_type=jnp.float32
                    )
                    for h in range(together):
                        one = projected[:, h * width : (h + 1) * width]
                        scale = lax.rsqrt(jnp.mean(one * one, axis=-1, keepdims=True) + EPS)
                        scale = jnp.where(kind < 2, scale, 1.0)
                        one = one * scale * gain_ref[start + h]
                        at = pl.ds((start + h) * width, width)
                        if tasks[t][0] == TEMPORAL:
                            out_refs[target][:, g, f, :, at] = one.reshape(split, part, width).astype(
                                jnp.bfloat16
                            )
                        else:
                            out_refs[target][:, at] = one.astype(jnp.bfloat16)

        for t in range(len(tasks)):
            if len(tasks) == 1:
                run(t)
            else:
                pl.when(step // 3 == t)(lambda t=t: run(t))

    outs = order.call(
        kernel,
        [*arrays, weights, gains],
        [pl.BlockSpec((row_count, depth), lambda j: (0, 0), pipeline_mode=pl.Buffered(1))]
        * len(arrays)
        + [
            pl.BlockSpec(
                (split, None, depth // split, columns),
                lambda j: (0, 3 * branch_at(j) + j % 3, 0, 0),
            ),
            pl.BlockSpec((None, None, heads, 1, width), lambda j: (branch_at(j), j % 3, 0, 0, 0)),
        ],
        out_specs,
        out_shape,
        6 * sum(map(len, writes)) * row_count * depth * columns * PROJECT_WEIGHT,
        ordered=True,
        grid=(3 * len(tasks),),
        name="project",
    )
    outs, found = list(outs), []
    for branch, groups in tasks:
        if branch == TEMPORAL:
            found.append(outs.pop(0))
        else:
            found.append([[outs.pop(0) for _ in group] for group in groups])
    return found


def temporal_attention(order, packed, heads, ordered):
    split, chunks, frames_each, patches, columns = packed.shape
    frames = split * frames_each
    width = columns // (3 * heads)
    group = min(patches, max(256 // frames, 8))
    unit = frames * group

    def kernel(x_ref, out_ref):
        row = lax.broadcasted_iota(jnp.int32, (unit, unit), 0)
        col = lax.broadcasted_iota(jnp.int32, (unit, unit), 1)
        seen = (row % group == col % group) & (col // group <= row // group)

        def read(c, first, kind, h):
            at = (kind * heads + h) * width
            piece = x_ref[:, c, :, first : first + group, at : at + width]
            if group % 16:
                return piece.astype(jnp.float32).reshape(unit, width).astype(jnp.bfloat16)
            return piece.reshape(unit, width)

        for c, first in itertools.product(range(chunks), range(0, patches, group)):
            for h in range(heads):
                q, k, v = (read(c, first, kind, h) for kind in range(3))
                scores = dot_transposed(q, k)
                scores = jnp.where(seen, scores, jnp.float32(-1e30))
                scores = jnp.exp(scores - jnp.max(scores, axis=-1, keepdims=True))
                total = jnp.sum(scores, axis=-1, keepdims=True)
                attended = jnp.dot(
                    scores.astype(jnp.bfloat16), v, preferred_element_type=jnp.float32
                )
                attended = (attended / total).reshape(split, frames_each, group, width)
                out_ref[:, c, :, first : first + group, h * width : (h + 1) * width] = (
                    attended.astype(jnp.bfloat16)
                )

    return order.call(
        kernel,
        [packed],
        [VMEM],
        [VMEM],
        [jax.ShapeDtypeStruct(packed.shape[:-1] + (heads * width,), jnp.bfloat16)],
        4 * unit * unit * width * heads * chunks * (patches // group) // LIGHT_WEIGHT,
        ordered=ordered,
        name="temporal_attention",
    )[0]


def finish_block(order, slot, frame, slots, temporal_out, w_out, table, arrived, heads, ordered):
    count = len(slots)
    row_count, columns = slots[0].shape
    columns //= 3
    width = columns // heads
    tiles_each = row_count // TILE
    listed = table.shape[1]
    split, _, depth, _ = w_out.shape
    part = temporal_out.shape[3]
    adds = arrived is not None

    def kernel(*refs):
        table_ref, slot_refs = refs[0], refs[1 : 1 + count]
        t_hbm, w_hbm = refs[1 + count], refs[2 + count]
        out_ref, q_ref, k_ref, v_ref, t_ref, w_ref, o_ref, sems = refs[3 + count + adds :][:8]

        copies = []

        def copy(source, target):
            copies.append(pltpu.make_async_copy(source, target, sems.at[len(copies)]))
            copies[-1].start()
            return copies[-1]

        first = [copy(slot_refs[slot].at[:, pl.ds(0, columns)], q_ref)]
        for s in range(count):
            at = pl.ds(s * row_count, row_count)
            first.append(copy(slot_refs[s].at[:, pl.ds(columns, columns)], k_ref.at[at]))
            first.append(copy(slot_refs[s].at[:, pl.ds(2 * columns, columns)], v_ref.at[at]))
        second = [copy(t_hbm.at[:, 0, frame], t_ref), copy(w_hbm, w_ref)]
        if adds:
            arrived_ref = refs[-1]
            second.append(copy(refs[3 + count], arrived_ref))
        for one in first:
            one.wait()
        for i in range(tiles_each):
            picks = [
                pl.ds(pl.multiple_of(table_ref[slot * tiles_each + i, j] * TILE, TILE), TILE)
                for j in range(listed)
            ]
            for h in range(heads):
                at = pl.ds(h * width, width)
                q = q_ref[pl.ds(i * TILE, TILE), at]
                k = jnp.concatenate([k_ref[p, at] for p in picks], axis=0)
                v = jnp.concatenate([v_ref[p, at] for p in picks], axis=0)
                scores = dot_transposed(q, k)
                scores = jnp.exp(scores - jnp.max(scores, axis=-1, keepdims=True))
                total = jnp.sum(scores, axis=-1, keepdims=True)
                attended = jnp.dot(
                    scores.astype(jnp.bfloat16), v, preferred_element_type=jnp.float32
                )
                o_ref[pl.ds(i * TILE, TILE), at] = (attended / total).astype(jnp.bfloat16)
        for one in second:
            one.wait()
        spatial = o_ref[...]
        temporal = t_ref[...]
        if part % 16:
            temporal = temporal.astype(jnp.float32)
        temporal = temporal.reshape(row_count, columns).astype(jnp.bfloat16)
        for s in range(split):
            at = pl.ds(s * depth, depth)
            value = dot_transposed(spatial, w_ref[s, 0]) + dot_transposed(temporal, w_ref[s, 1])
            if adds:
                value += arrived_ref[:, at].astype(jnp.float32)
            out_ref[:, at] = value.astype(jnp.bfloat16)

    operands = [table, *slots, temporal_out, w_out] + [arrived] * adds
    held = (row_count, split * depth)
    scratch = [
        pltpu.VMEM((row_count, columns), jnp.bfloat16),
        pltpu.VMEM((count * row_count, columns), jnp.bfloat16),
        pltpu.VMEM((count * row_count, columns), jnp.bfloat16),
        pltpu.VMEM((split, part, columns), jnp.bfloat16),
        pltpu.VMEM((split, 2, depth, columns), jnp.bfloat16),
        pltpu.VMEM((row_count, columns), jnp.bfloat16),
        pltpu.SemaphoreType.DMA((2 * count + 4,)),
    ]
    return order.call(
        kernel,
        operands,
        [pl.BlockSpec(memory_space=pltpu.SMEM)] + [ANY] * (len(operands) - 1),
        [VMEM],
        [jax.ShapeDtypeStruct(held, jnp.bfloat16)],
        (4 * row_count * listed * TILE * columns + 4 * row_count * columns * split * depth)
        // LIGHT_WEIGHT,
        ordered=ordered,
        scratch_shapes=scratch + [pltpu.VMEM(held, jnp.bfloat16)] * adds,
        name="finish_block",
    )[0]


def slot_order(window_blocks, me, ring, tiles_each):
    def renumber(tile):
        return (me - tile // tiles_each + ring) % ring * tiles_each + tile % tiles_each

    rows = renumber(jnp.arange(ring * tiles_each, dtype=jnp.int32))
    return renumber(window_blocks[rows])


def body(tokens, norm_gain, qk_gain, window_blocks, w_spatial, w_temporal, w_out):
    rows_here, frames_here, _ = tokens.shape
    heads, width = qk_gain.shape[2:]
    ring = lax.axis_size("grp")
    me = lax.axis_index("grp")
    forward = [(i, (i + 1) % ring) for i in range(ring)]
    order = Order()

    def send(arrays):
        return [lax.ppermute(x, "grp", forward) for x in arrays]

    def swap(array):
        return lax.all_to_all(array, "seq", split_axis=0, concat_axis=0, tiled=True)

    wide = tokens.astype(jnp.float32)
    normed = (
        wide * lax.rsqrt(jnp.mean(wide * wide, axis=-1, keepdims=True) + EPS) * norm_gain
    ).astype(jnp.bfloat16)
    normed, w_spatial, w_temporal = lax.optimization_barrier((normed, w_spatial, w_temporal))
    full_qkv = lax.all_gather(
        jnp.concatenate([w_spatial.transpose(1, 0, 2), w_temporal.transpose(1, 0, 2)]),
        "seq",
        axis=0,
    )
    full_out = lax.all_gather(w_out.transpose(1, 0, 2), "seq", axis=0)
    gains = jnp.concatenate([qk_gain, jnp.ones_like(qk_gain[:, :1])], axis=1)
    gains = gains * jnp.array([width**-0.5, 1.0, 1.0], jnp.float32)[None, :, None, None]
    gains = gains[:, :, :, None, :]
    table = slot_order(window_blocks, me, ring, rows_here // TILE)

    def temporal(k):
        (packed,) = project(order, [(TEMPORAL, [chunks[k]])], full_qkv, gains)
        exchanged[k] = swap(packed)

    def attend(k, ordered=False):
        temporal_outs[k] = swap(temporal_attention(order, exchanged[k], heads, ordered))

    def spatial(ks):
        tasks = [(SPATIAL, [chunks[k] for k in ks])]
        slots.update(zip(ks, project(order, tasks, full_qkv, gains)[0]))

    def finish(slot, frame, arrived, ordered=False):
        return finish_block(
            order,
            slot,
            frame,
            [slots[k][frame] for k in range(ring)],
            temporal_outs[slot],
            full_out,
            table,
            arrived,
            heads,
            ordered,
        )

    last = ring - 1
    chunks = [[normed[:, f] for f in range(frames_here)]]
    chunks += [[None] * frames_here for _ in range(last)]
    slots, exchanged, temporal_outs, arrived, sums = {}, {}, {}, {}, []
    for window in range(last + frames_here - 1):
        if arrived:
            for (k, f), x in zip(arrived, relay(order, list(arrived.values()))):
                chunks[k][f] = x
        steps = [window + 1 - f for f in range(frames_here)]
        moving = [(k, f) for f, k in enumerate(steps) if 1 <= k <= last]
        arrived = {(k, f): send([chunks[k - 1][f]])[0] for k, f in moving}
        ready = window - frames_here + 1
        if ready == 1 and last > 1:
            temporal(1)
            ahead = chunks[2][: frames_here - 1] if last > 2 else []
            groups = [chunks[1], chunks[0]] + ([ahead] if ahead else [])
            found = project(order, [(SPATIAL, groups)], full_qkv, gains)[0]
            slots[1], slots[0] = found[:2]
            if ahead:
                slots[2] = found[2]
            temporal(0)
            attend(1, True)
        elif ready > 0:
            at_end = ready == last - 1
            some = chunks[last][:-1] if at_end and frames_here > 1 else []
            have = slots.setdefault(ready, [])
            tasks = [
                (SPATIAL, [chunks[ready][len(have) :]] + ([some] if some else [])),
                (TEMPORAL, [chunks[ready]]),
            ]
            found = project(order, tasks, full_qkv, gains)
            slots[ready], exchanged[ready] = have + found[0][0], swap(found[1])
            if some:
                slots[last] = found[0][1]
                sums = [finish(1, f, None, True) for f in range(len(some))]
    for (k, f), x in arrived.items():
        chunks[k][f] = x
    if last == 1:
        temporal(1)
        spatial([0])
        temporal(0)
        attend(1, True)
    have = slots.setdefault(last, [])
    tasks = [(SPATIAL, [chunks[last][len(have) :]])]
    if last > 1:
        tasks += [(TEMPORAL, [chunks[last]])]
    found = project(order, tasks, full_qkv, gains)
    have += found[0][0]
    if last > 1:
        exchanged[last] = swap(found[1])
    sums = send(sums + [finish(1, f, None, True) for f in range(len(sums), frames_here)])
    for k in range(1, ring):
        if k not in temporal_outs and k < last:
            attend(k, True)
    for k in range(ring):
        if k not in temporal_outs:
            attend(k)
    for slot in range(2, ring):
        sums = send([finish(slot, f, sums[f]) for f in range(frames_here)])
    own = [finish(0, f, None) for f in range(frames_here)]
    total = jnp.stack(
        [o.astype(jnp.float32) + s.astype(jnp.float32) for o, s in zip(own, sums)], axis=1
    )
    return (wide + total).astype(jnp.bfloat16)


def solution(mesh):
    return jax.shard_map(
        body,
        mesh=mesh,
        in_specs=(
            P("grp", "seq", None),
            P(),
            P(None, None, "grp", None),
            P(),
            P("seq", None, "grp"),
            P("seq", None, "grp"),
            P("seq", None, "grp"),
        ),
        out_specs=P("grp", "seq", None),
        check_vma=False,
    )
```

```python
import itertools

import jax
import jax.numpy as jnp
from jax import lax
from jax.experimental import pallas as pl
from jax.experimental.pallas import tpu as pltpu
from jax.sharding import PartitionSpec as P

TILE = 128
PROJECT_WEIGHT, LIGHT_WEIGHT = 3, 10
EPS = 1e-06
VMEM_BYTES = 56 * 1024 * 1024
VMEM = pl.BlockSpec(memory_space=pltpu.VMEM)
ANY = pl.BlockSpec(memory_space=pl.ANY)
MARK = jax.ShapeDtypeStruct((8, 128), jnp.float32)


def params():
    return pltpu.CompilerParams(vmem_limit_bytes=VMEM_BYTES)


def dot_transposed(a, b):
    return lax.dot_general(a, b, (((1,), (1,)), ((), ())), preferred_element_type=jnp.float32)


class Order:
    def __init__(self):
        self.mark = None

    def call(self, kernel, operands, in_specs, out_specs, out_shape, flops, ordered=False, **more):
        count = len(operands)
        marked = ordered and self.mark is not None

        def run(*refs):
            rest = refs[count + marked :]
            kernel(*refs[:count], *rest[: len(out_shape)], *rest[len(out_shape) + ordered :])

        outs = pl.pallas_call(
            run,
            in_specs=in_specs + [ANY] * marked,
            out_specs=out_specs + [ANY] * ordered,
            out_shape=out_shape + [MARK] * ordered,
            compiler_params=params(),
            cost_estimate=pl.CostEstimate(flops=flops, bytes_accessed=0, transcendentals=0),
            **more,
        )(*operands, *([self.mark] * marked))
        if ordered:
            *outs, self.mark = outs
        return outs


def relay(order, arrays):
    return order.call(
        lambda *refs: None,
        arrays,
        [ANY] * len(arrays),
        [ANY] * len(arrays),
        [jax.ShapeDtypeStruct(x.shape, x.dtype) for x in arrays],
        0,
        ordered=True,
        input_output_aliases={i: i for i in range(len(arrays))},
        name="relay",
    )


SPATIAL, TEMPORAL = 0, 1


def project(order, tasks, weights, gains):
    arrays = []
    for _, groups in tasks:
        arrays += [x for group in groups for x in group if not any(x is y for y in arrays)]
    row_count, depth = arrays[0].shape
    split, _, _, columns = weights.shape
    heads, width = gains.shape[2], gains.shape[4]
    part = row_count // split
    together = max(1, min(heads, 256 // width))
    span = together * width

    def index(x):
        return [y is x for y in arrays].index(True)

    def branch_at(j):
        found = tasks[0][0]
        for t in range(1, len(tasks)):
            found = jnp.where(j >= 3 * t, tasks[t][0], found)
        return found

    out_shape, out_specs, writes = [], [], []
    for t, (branch, groups) in enumerate(tasks):

        def place(j, t=t):
            return jnp.clip(j - 3 * t, 0, 2)

        writes.append([])
        for g, group in enumerate(groups):
            frames = len(group)
            for f, x in enumerate(group):
                first = len(out_shape) + (f if branch == SPATIAL else 0)
                writes[-1].append((index(x), first, g, f))
            if branch == SPATIAL:
                out_shape += [jax.ShapeDtypeStruct((row_count, 3 * columns), jnp.bfloat16)] * frames
                out_specs += [
                    pl.BlockSpec((row_count, columns), lambda j, place=place: (0, place(j)))
                ] * frames
        if branch == TEMPORAL:
            whole = (split, len(groups), len(groups[0]), part, 3 * columns)
            out_shape.append(jax.ShapeDtypeStruct(whole, jnp.bfloat16))
            out_specs.append(
                pl.BlockSpec(
                    whole[:-1] + (columns,), lambda j, place=place: (0, 0, 0, 0, place(j))
                )
            )

    def kernel(*refs):
        row_refs, w_ref, gain_ref = refs[: len(arrays)], refs[len(arrays)], refs[len(arrays) + 1]
        out_refs = refs[len(arrays) + 2 :]
        step = pl.program_id(0)
        kind = step % 3

        def run(t):
            for start in range(0, heads, together):
                w = w_ref[:, :, start * width : start * width + span].reshape(depth, span)
                for source, target, g, f in writes[t]:
                    projected = jnp.dot(
                        row_refs[source][...], w, preferred_element_type=jnp.float32
                    )
                    for h in range(together):
                        one = projected[:, h * width : (h + 1) * width]
                        scale = lax.rsqrt(jnp.mean(one * one, axis=-1, keepdims=True) + EPS)
                        scale = jnp.where(kind < 2, scale, 1.0)
                        one = one * scale * gain_ref[start + h]
                        at = pl.ds((start + h) * width, width)
                        if tasks[t][0] == TEMPORAL:
                            out_refs[target][:, g, f, :, at] = one.reshape(split, part, width).astype(
                                jnp.bfloat16
                            )
                        else:
                            out_refs[target][:, at] = one.astype(jnp.bfloat16)

        for t in range(len(tasks)):
            if len(tasks) == 1:
                run(t)
            else:
                pl.when(step // 3 == t)(lambda t=t: run(t))

    outs = order.call(
        kernel,
        [*arrays, weights, gains],
        [pl.BlockSpec((row_count, depth), lambda j: (0, 0), pipeline_mode=pl.Buffered(1))]
        * len(arrays)
        + [
            pl.BlockSpec(
                (split, None, depth // split, columns),
                lambda j: (0, 3 * branch_at(j) + j % 3, 0, 0),
            ),
            pl.BlockSpec((None, None, heads, 1, width), lambda j: (branch_at(j), j % 3, 0, 0, 0)),
        ],
        out_specs,
        out_shape,
        6 * sum(map(len, writes)) * row_count * depth * columns * PROJECT_WEIGHT,
        ordered=True,
        grid=(3 * len(tasks),),
        name="project",
    )
    outs, found = list(outs), []
    for branch, groups in tasks:
        if branch == TEMPORAL:
            found.append(outs.pop(0))
        else:
            found.append([[outs.pop(0) for _ in group] for group in groups])
    return found


def temporal_attention(order, packed, heads, ordered):
    split, chunks, frames_each, patches, columns = packed.shape
    frames = split * frames_each
    width = columns // (3 * heads)
    group = min(patches, max(256 // frames, 8))
    unit = frames * group

    def kernel(x_ref, out_ref):
        row = lax.broadcasted_iota(jnp.int32, (unit, unit), 0)
        col = lax.broadcasted_iota(jnp.int32, (unit, unit), 1)
        seen = (row % group == col % group) & (col // group <= row // group)

        def read(c, first, kind, h):
            at = (kind * heads + h) * width
            piece = x_ref[:, c, :, first : first + group, at : at + width]
            if group % 16:
                return piece.astype(jnp.float32).reshape(unit, width).astype(jnp.bfloat16)
            return piece.reshape(unit, width)

        for c, first in itertools.product(range(chunks), range(0, patches, group)):
            for h in range(heads):
                q, k, v = (read(c, first, kind, h) for kind in range(3))
                scores = dot_transposed(q, k)
                scores = jnp.where(seen, scores, jnp.float32(-1e30))
                scores = jnp.exp(scores - jnp.max(scores, axis=-1, keepdims=True))
                total = jnp.sum(scores, axis=-1, keepdims=True)
                attended = jnp.dot(
                    scores.astype(jnp.bfloat16), v, preferred_element_type=jnp.float32
                )
                attended = (attended / total).reshape(split, frames_each, group, width)
                out_ref[:, c, :, first : first + group, h * width : (h + 1) * width] = (
                    attended.astype(jnp.bfloat16)
                )

    return order.call(
        kernel,
        [packed],
        [VMEM],
        [VMEM],
        [jax.ShapeDtypeStruct(packed.shape[:-1] + (heads * width,), jnp.bfloat16)],
        4 * unit * unit * width * heads * chunks * (patches // group) // LIGHT_WEIGHT,
        ordered=ordered,
        name="temporal_attention",
    )[0]


def finish_block(order, slot, frame, slots, temporal_out, w_out, table, arrived, heads, ordered):
    count = len(slots)
    row_count, columns = slots[0].shape
    columns //= 3
    width = columns // heads
    tiles_each = row_count // TILE
    listed = table.shape[1]
    split, _, depth, _ = w_out.shape
    part = temporal_out.shape[3]
    adds = arrived is not None

    def kernel(*refs):
        table_ref, slot_refs = refs[0], refs[1 : 1 + count]
        t_hbm, w_hbm = refs[1 + count], refs[2 + count]
        out_ref, q_ref, k_ref, v_ref, t_ref, w_ref, o_ref, sems = refs[3 + count + adds :][:8]

        copies = []

        def copy(source, target):
            copies.append(pltpu.make_async_copy(source, target, sems.at[len(copies)]))
            copies[-1].start()
            return copies[-1]

        first = [copy(slot_refs[slot].at[:, pl.ds(0, columns)], q_ref)]
        for s in range(count):
            at = pl.ds(s * row_count, row_count)
            first.append(copy(slot_refs[s].at[:, pl.ds(columns, columns)], k_ref.at[at]))
            first.append(copy(slot_refs[s].at[:, pl.ds(2 * columns, columns)], v_ref.at[at]))
        second = [copy(t_hbm.at[:, 0, frame], t_ref), copy(w_hbm, w_ref)]
        if adds:
            arrived_ref = refs[-1]
            second.append(copy(refs[3 + count], arrived_ref))
        for one in first:
            one.wait()
        for i in range(tiles_each):
            picks = [
                pl.ds(pl.multiple_of(table_ref[slot * tiles_each + i, j] * TILE, TILE), TILE)
                for j in range(listed)
            ]
            cuts = [pl.ds(h * width, width) for h in range(heads)]
            scores = [
                dot_transposed(
                    q_ref[pl.ds(i * TILE, TILE), at],
                    jnp.concatenate([k_ref[p, at] for p in picks], axis=0),
                )
                for at in cuts
            ]
            scores = [jnp.exp(x - jnp.max(x, axis=-1, keepdims=True)) for x in scores]
            totals = [jnp.sum(x, axis=-1, keepdims=True) for x in scores]
            for at, x, total in zip(cuts, scores, totals):
                v = jnp.concatenate([v_ref[p, at] for p in picks], axis=0)
                attended = jnp.dot(x.astype(jnp.bfloat16), v, preferred_element_type=jnp.float32)
                o_ref[pl.ds(i * TILE, TILE), at] = (attended / total).astype(jnp.bfloat16)
        for one in second:
            one.wait()
        spatial = o_ref[...]
        temporal = t_ref[...]
        if part % 16:
            temporal = temporal.astype(jnp.float32)
        temporal = temporal.reshape(row_count, columns).astype(jnp.bfloat16)
        for s in range(split):
            at = pl.ds(s * depth, depth)
            value = dot_transposed(spatial, w_ref[s, 0]) + dot_transposed(temporal, w_ref[s, 1])
            if adds:
                value += arrived_ref[:, at].astype(jnp.float32)
            out_ref[:, at] = value.astype(jnp.bfloat16)

    operands = [table, *slots, temporal_out, w_out] + [arrived] * adds
    held = (row_count, split * depth)
    scratch = [
        pltpu.VMEM((row_count, columns), jnp.bfloat16),
        pltpu.VMEM((count * row_count, columns), jnp.bfloat16),
        pltpu.VMEM((count * row_count, columns), jnp.bfloat16),
        pltpu.VMEM((split, part, columns), jnp.bfloat16),
        pltpu.VMEM((split, 2, depth, columns), jnp.bfloat16),
        pltpu.VMEM((row_count, columns), jnp.bfloat16),
        pltpu.SemaphoreType.DMA((2 * count + 4,)),
    ]
    return order.call(
        kernel,
        operands,
        [pl.BlockSpec(memory_space=pltpu.SMEM)] + [ANY] * (len(operands) - 1),
        [VMEM],
        [jax.ShapeDtypeStruct(held, jnp.bfloat16)],
        (4 * row_count * listed * TILE * columns + 4 * row_count * columns * split * depth)
        // LIGHT_WEIGHT,
        ordered=ordered,
        scratch_shapes=scratch + [pltpu.VMEM(held, jnp.bfloat16)] * adds,
        name="finish_block",
    )[0]


def slot_order(window_blocks, me, ring, tiles_each):
    def renumber(tile):
        return (me - tile // tiles_each + ring) % ring * tiles_each + tile % tiles_each

    rows = renumber(jnp.arange(ring * tiles_each, dtype=jnp.int32))
    return renumber(window_blocks[rows])


def body(tokens, norm_gain, qk_gain, window_blocks, w_spatial, w_temporal, w_out):
    rows_here, frames_here, _ = tokens.shape
    heads, width = qk_gain.shape[2:]
    ring = lax.axis_size("grp")
    me = lax.axis_index("grp")
    forward = [(i, (i + 1) % ring) for i in range(ring)]
    order = Order()

    def send(arrays):
        return [lax.ppermute(x, "grp", forward) for x in arrays]

    def swap(array):
        return lax.all_to_all(array, "seq", split_axis=0, concat_axis=0, tiled=True)

    wide = tokens.astype(jnp.float32)
    normed = (
        wide * lax.rsqrt(jnp.mean(wide * wide, axis=-1, keepdims=True) + EPS) * norm_gain
    ).astype(jnp.bfloat16)
    full_qkv = lax.all_gather(
        jnp.concatenate([w_spatial.transpose(1, 0, 2), w_temporal.transpose(1, 0, 2)]),
        "seq",
        axis=0,
    )
    full_out = lax.all_gather(w_out.transpose(1, 0, 2), "seq", axis=0)
    gains = jnp.concatenate([qk_gain, jnp.ones_like(qk_gain[:, :1])], axis=1)
    gains = gains * jnp.array([width**-0.5, 1.0, 1.0], jnp.float32)[None, :, None, None]
    gains = gains[:, :, :, None, :]
    table = slot_order(window_blocks, me, ring, rows_here // TILE)

    def temporal(k):
        (packed,) = project(order, [(TEMPORAL, [chunks[k]])], full_qkv, gains)
        exchanged[k] = swap(packed)

    def attend(k, ordered=False):
        temporal_outs[k] = swap(temporal_attention(order, exchanged[k], heads, ordered))

    def spatial(ks):
        tasks = [(SPATIAL, [chunks[k] for k in ks])]
        slots.update(zip(ks, project(order, tasks, full_qkv, gains)[0]))

    def finish(slot, frame, arrived, ordered=False):
        return finish_block(
            order,
            slot,
            frame,
            [slots[k][frame] for k in range(ring)],
            temporal_outs[slot],
            full_out,
            table,
            arrived,
            heads,
            ordered,
        )

    last = ring - 1
    chunks = [[normed[:, f] for f in range(frames_here)]]
    chunks += [[None] * frames_here for _ in range(last)]
    slots, exchanged, temporal_outs, arrived, sums = {}, {}, {}, {}, []
    for window in range(last + frames_here - 1):
        if arrived:
            for (k, f), x in zip(arrived, relay(order, list(arrived.values()))):
                chunks[k][f] = x
        steps = [window + 1 - f for f in range(frames_here)]
        moving = [(k, f) for f, k in enumerate(steps) if 1 <= k <= last]
        arrived = {(k, f): send([chunks[k - 1][f]])[0] for k, f in moving}
        ready = window - frames_here + 1
        if ready == 1 and last > 1:
            temporal(1)
            ahead = chunks[2][: frames_here - 1] if last > 2 else []
            groups = [chunks[1], chunks[0]] + ([ahead] if ahead else [])
            found = project(order, [(SPATIAL, groups)], full_qkv, gains)[0]
            slots[1], slots[0] = found[:2]
            if ahead:
                slots[2] = found[2]
            temporal(0)
            attend(1, True)
        elif ready > 0:
            at_end = ready == last - 1
            some = chunks[last][:-1] if at_end and frames_here > 1 else []
            have = slots.setdefault(ready, [])
            tasks = [
                (SPATIAL, [chunks[ready][len(have) :]] + ([some] if some else [])),
                (TEMPORAL, [chunks[ready]]),
            ]
            found = project(order, tasks, full_qkv, gains)
            slots[ready], exchanged[ready] = have + found[0][0], swap(found[1])
            if some:
                slots[last] = found[0][1]
                sums = [finish(1, f, None, True) for f in range(len(some))]
    for (k, f), x in arrived.items():
        chunks[k][f] = x
    if last == 1:
        temporal(1)
        spatial([0])
        temporal(0)
        attend(1, True)
    have = slots.setdefault(last, [])
    tasks = [(SPATIAL, [chunks[last][len(have) :]])]
    if last > 1:
        tasks += [(TEMPORAL, [chunks[last]])]
    found = project(order, tasks, full_qkv, gains)
    have += found[0][0]
    if last > 1:
        exchanged[last] = swap(found[1])
    sums = send(sums + [finish(1, f, None, True) for f in range(len(sums), frames_here)])
    for k in range(1, ring):
        if k not in temporal_outs and k < last:
            attend(k, True)
    for k in range(ring):
        if k not in temporal_outs:
            attend(k)
    for slot in range(2, ring):
        sums = send([finish(slot, f, sums[f]) for f in range(frames_here)])
    own = [finish(0, f, None) for f in range(frames_here)]
    total = jnp.stack(
        [o.astype(jnp.float32) + s.astype(jnp.float32) for o, s in zip(own, sums)], axis=1
    )
    return (wide + total).astype(jnp.bfloat16)


def solution(mesh):
    return jax.shard_map(
        body,
        mesh=mesh,
        in_specs=(
            P("grp", "seq", None),
            P(),
            P(None, None, "grp", None),
            P(),
            P("seq", None, "grp"),
            P("seq", None, "grp"),
            P("seq", None, "grp"),
        ),
        out_specs=P("grp", "seq", None),
        check_vma=False,
    )
```

```python
import itertools

import jax
import jax.numpy as jnp
from jax import lax
from jax.experimental import pallas as pl
from jax.experimental.pallas import tpu as pltpu
from jax.sharding import PartitionSpec as P

TILE = 128
PROJECT_WEIGHT, LIGHT_WEIGHT = 3, 10
EPS = 1e-06
VMEM_BYTES = 56 * 1024 * 1024
VMEM = pl.BlockSpec(memory_space=pltpu.VMEM)
ANY = pl.BlockSpec(memory_space=pl.ANY)
MARK = jax.ShapeDtypeStruct((8, 128), jnp.float32)


def params():
    return pltpu.CompilerParams(vmem_limit_bytes=VMEM_BYTES)


def dot_transposed(a, b):
    return lax.dot_general(a, b, (((1,), (1,)), ((), ())), preferred_element_type=jnp.float32)


class Order:
    def __init__(self):
        self.mark = None

    def call(self, kernel, operands, in_specs, out_specs, out_shape, flops, ordered=False, **more):
        count = len(operands)
        marked = ordered and self.mark is not None

        def run(*refs):
            rest = refs[count + marked :]
            kernel(*refs[:count], *rest[: len(out_shape)], *rest[len(out_shape) + ordered :])

        outs = pl.pallas_call(
            run,
            in_specs=in_specs + [ANY] * marked,
            out_specs=out_specs + [ANY] * ordered,
            out_shape=out_shape + [MARK] * ordered,
            compiler_params=params(),
            cost_estimate=pl.CostEstimate(flops=flops, bytes_accessed=0, transcendentals=0),
            **more,
        )(*operands, *([self.mark] * marked))
        if ordered:
            *outs, self.mark = outs
        return outs


def relay(order, arrays):
    return order.call(
        lambda *refs: None,
        arrays,
        [ANY] * len(arrays),
        [ANY] * len(arrays),
        [jax.ShapeDtypeStruct(x.shape, x.dtype) for x in arrays],
        0,
        ordered=True,
        input_output_aliases={i: i for i in range(len(arrays))},
        name="relay",
    )


SPATIAL, TEMPORAL = 0, 1


def project(order, tasks, weights, gains):
    arrays = []
    for _, groups in tasks:
        arrays += [x for group in groups for x in group if not any(x is y for y in arrays)]
    row_count, depth = arrays[0].shape
    split, _, _, columns = weights.shape
    heads, width = gains.shape[2], gains.shape[4]
    part = row_count // split
    together = max(1, min(heads, 256 // width))
    span = together * width

    def index(x):
        return [y is x for y in arrays].index(True)

    def branch_at(j):
        found = tasks[0][0]
        for t in range(1, len(tasks)):
            found = jnp.where(j >= 3 * t, tasks[t][0], found)
        return found

    out_shape, out_specs, writes = [], [], []
    for t, (branch, groups) in enumerate(tasks):

        def place(j, t=t):
            return jnp.clip(j - 3 * t, 0, 2)

        writes.append([])
        for g, group in enumerate(groups):
            frames = len(group)
            for f, x in enumerate(group):
                first = len(out_shape) + (f if branch == SPATIAL else 0)
                writes[-1].append((index(x), first, g, f))
            if branch == SPATIAL:
                out_shape += [jax.ShapeDtypeStruct((row_count, 3 * columns), jnp.bfloat16)] * frames
                out_specs += [
                    pl.BlockSpec((row_count, columns), lambda j, place=place: (0, place(j)))
                ] * frames
        if branch == TEMPORAL:
            whole = (split, len(groups), len(groups[0]), part, 3 * columns)
            out_shape.append(jax.ShapeDtypeStruct(whole, jnp.bfloat16))
            out_specs.append(
                pl.BlockSpec(
                    whole[:-1] + (columns,), lambda j, place=place: (0, 0, 0, 0, place(j))
                )
            )

    def kernel(*refs):
        row_refs, w_ref, gain_ref = refs[: len(arrays)], refs[len(arrays)], refs[len(arrays) + 1]
        out_refs = refs[len(arrays) + 2 :]
        step = pl.program_id(0)
        kind = step % 3

        def run(t):
            for start in range(0, heads, together):
                w = w_ref[:, :, start * width : start * width + span].reshape(depth, span)
                for source, target, g, f in writes[t]:
                    projected = jnp.dot(
                        row_refs[source][...], w, preferred_element_type=jnp.float32
                    )
                    for h in range(together):
                        one = projected[:, h * width : (h + 1) * width]
                        scale = lax.rsqrt(jnp.mean(one * one, axis=-1, keepdims=True) + EPS)
                        scale = jnp.where(kind < 2, scale, 1.0)
                        one = one * scale * gain_ref[start + h]
                        at = pl.ds((start + h) * width, width)
                        if tasks[t][0] == TEMPORAL:
                            out_refs[target][:, g, f, :, at] = one.reshape(split, part, width).astype(
                                jnp.bfloat16
                            )
                        else:
                            out_refs[target][:, at] = one.astype(jnp.bfloat16)

        for t in range(len(tasks)):
            if len(tasks) == 1:
                run(t)
            else:
                pl.when(step // 3 == t)(lambda t=t: run(t))

    outs = order.call(
        kernel,
        [*arrays, weights, gains],
        [pl.BlockSpec((row_count, depth), lambda j: (0, 0), pipeline_mode=pl.Buffered(1))]
        * len(arrays)
        + [
            pl.BlockSpec(
                (split, None, depth // split, columns),
                lambda j: (0, 3 * branch_at(j) + j % 3, 0, 0),
            ),
            pl.BlockSpec((None, None, heads, 1, width), lambda j: (branch_at(j), j % 3, 0, 0, 0)),
        ],
        out_specs,
        out_shape,
        6 * sum(map(len, writes)) * row_count * depth * columns * PROJECT_WEIGHT,
        ordered=True,
        grid=(3 * len(tasks),),
        name="project",
    )
    outs, found = list(outs), []
    for branch, groups in tasks:
        if branch == TEMPORAL:
            found.append(outs.pop(0))
        else:
            found.append([[outs.pop(0) for _ in group] for group in groups])
    return found


def temporal_attention(order, packed, heads, ordered):
    split, chunks, frames_each, patches, columns = packed.shape
    frames = split * frames_each
    width = columns // (3 * heads)
    group = min(patches, max(256 // frames, 8))
    unit = frames * group

    def kernel(x_ref, out_ref):
        row = lax.broadcasted_iota(jnp.int32, (unit, unit), 0)
        col = lax.broadcasted_iota(jnp.int32, (unit, unit), 1)
        seen = (row % group == col % group) & (col // group <= row // group)

        def read(c, first, kind, h):
            at = (kind * heads + h) * width
            piece = x_ref[:, c, :, first : first + group, at : at + width]
            if group % 16:
                return piece.astype(jnp.float32).reshape(unit, width).astype(jnp.bfloat16)
            return piece.reshape(unit, width)

        for c, first in itertools.product(range(chunks), range(0, patches, group)):
            for h in range(heads):
                q, k, v = (read(c, first, kind, h) for kind in range(3))
                scores = dot_transposed(q, k)
                scores = jnp.where(seen, scores, jnp.float32(-1e30))
                scores = jnp.exp(scores - jnp.max(scores, axis=-1, keepdims=True))
                total = jnp.sum(scores, axis=-1, keepdims=True)
                attended = jnp.dot(
                    scores.astype(jnp.bfloat16), v, preferred_element_type=jnp.float32
                )
                attended = (attended / total).reshape(split, frames_each, group, width)
                out_ref[:, c, :, first : first + group, h * width : (h + 1) * width] = (
                    attended.astype(jnp.bfloat16)
                )

    return order.call(
        kernel,
        [packed],
        [VMEM],
        [VMEM],
        [jax.ShapeDtypeStruct(packed.shape[:-1] + (heads * width,), jnp.bfloat16)],
        4 * unit * unit * width * heads * chunks * (patches // group) // LIGHT_WEIGHT,
        ordered=ordered,
        name="temporal_attention",
    )[0]


def finish_block(order, slot, frame, slots, temporal_out, w_out, table, arrived, heads, ordered):
    count = len(slots)
    row_count, columns = slots[0].shape
    columns //= 3
    width = columns // heads
    tiles_each = row_count // TILE
    listed = table.shape[1]
    split, _, depth, _ = w_out.shape
    part = temporal_out.shape[3]
    adds = arrived is not None

    def kernel(*refs):
        table_ref, slot_refs = refs[0], refs[1 : 1 + count]
        t_hbm, w_hbm = refs[1 + count], refs[2 + count]
        out_ref, q_ref, k_ref, v_ref, t_ref, w_ref, o_ref, sems = refs[3 + count + adds :][:8]

        copies = []

        def copy(source, target):
            copies.append(pltpu.make_async_copy(source, target, sems.at[len(copies)]))
            copies[-1].start()
            return copies[-1]

        first = [copy(slot_refs[slot].at[:, pl.ds(0, columns)], q_ref)]
        for s in range(count):
            at = pl.ds(s * row_count, row_count)
            first.append(copy(slot_refs[s].at[:, pl.ds(columns, columns)], k_ref.at[at]))
            first.append(copy(slot_refs[s].at[:, pl.ds(2 * columns, columns)], v_ref.at[at]))
        second = [copy(t_hbm.at[:, 0, frame], t_ref), copy(w_hbm, w_ref)]
        if adds:
            arrived_ref = refs[-1]
            second.append(copy(refs[3 + count], arrived_ref))
        for one in first:
            one.wait()
        for i in range(tiles_each):
            picks = [
                pl.ds(pl.multiple_of(table_ref[slot * tiles_each + i, j] * TILE, TILE), TILE)
                for j in range(listed)
            ]
            cuts = [pl.ds(h * width, width) for h in range(heads)]
            scores = [
                dot_transposed(
                    q_ref[pl.ds(i * TILE, TILE), at],
                    jnp.concatenate([k_ref[p, at] for p in picks], axis=0),
                )
                for at in cuts
            ]
            scores = [jnp.exp(x - jnp.max(x, axis=-1, keepdims=True)) for x in scores]
            totals = [jnp.sum(x, axis=-1, keepdims=True) for x in scores]
            for at, x, total in zip(cuts, scores, totals):
                v = jnp.concatenate([v_ref[p, at] for p in picks], axis=0)
                attended = jnp.dot(x.astype(jnp.bfloat16), v, preferred_element_type=jnp.float32)
                o_ref[pl.ds(i * TILE, TILE), at] = (attended / total).astype(jnp.bfloat16)
        for one in second:
            one.wait()
        spatial = o_ref[...]
        temporal = t_ref[...]
        if part % 16:
            temporal = temporal.astype(jnp.float32)
        temporal = temporal.reshape(row_count, columns).astype(jnp.bfloat16)
        for s in range(split):
            at = pl.ds(s * depth, depth)
            value = dot_transposed(spatial, w_ref[s, 0]) + dot_transposed(temporal, w_ref[s, 1])
            if adds:
                value += arrived_ref[:, at].astype(jnp.float32)
            out_ref[:, at] = value.astype(jnp.bfloat16)

    operands = [table, *slots, temporal_out, w_out] + [arrived] * adds
    held = (row_count, split * depth)
    scratch = [
        pltpu.VMEM((row_count, columns), jnp.bfloat16),
        pltpu.VMEM((count * row_count, columns), jnp.bfloat16),
        pltpu.VMEM((count * row_count, columns), jnp.bfloat16),
        pltpu.VMEM((split, part, columns), jnp.bfloat16),
        pltpu.VMEM((split, 2, depth, columns), jnp.bfloat16),
        pltpu.VMEM((row_count, columns), jnp.bfloat16),
        pltpu.SemaphoreType.DMA((2 * count + 4,)),
    ]
    return order.call(
        kernel,
        operands,
        [pl.BlockSpec(memory_space=pltpu.SMEM)] + [ANY] * (len(operands) - 1),
        [VMEM],
        [jax.ShapeDtypeStruct(held, jnp.bfloat16)],
        (4 * row_count * listed * TILE * columns + 4 * row_count * columns * split * depth)
        // LIGHT_WEIGHT,
        ordered=ordered,
        scratch_shapes=scratch + [pltpu.VMEM(held, jnp.bfloat16)] * adds,
        name="finish_block",
    )[0]


def combine(tokens, own, sums):
    row_count, frames, depth = tokens.shape
    block = min(row_count, 64)

    def kernel(t_ref, *refs):
        out_ref = refs[-1]
        for f in range(frames):
            total = refs[f][...].astype(jnp.float32) + refs[frames + f][...].astype(jnp.float32)
            out_ref[:, f, :] = (t_ref[:, f, :].astype(jnp.float32) + total).astype(jnp.bfloat16)

    rows = pl.BlockSpec((block, depth), lambda i: (i, 0))
    whole = pl.BlockSpec((block, frames, depth), lambda i: (i, 0, 0))
    return pl.pallas_call(
        kernel,
        grid=(row_count // block,),
        in_specs=[whole] + [rows] * (2 * frames),
        out_specs=whole,
        out_shape=jax.ShapeDtypeStruct(tokens.shape, tokens.dtype),
        compiler_params=params(),
        name="combine",
    )(tokens, *own, *sums)


def slot_order(window_blocks, me, ring, tiles_each):
    def renumber(tile):
        return (me - tile // tiles_each + ring) % ring * tiles_each + tile % tiles_each

    rows = renumber(jnp.arange(ring * tiles_each, dtype=jnp.int32))
    return renumber(window_blocks[rows])


def body(tokens, norm_gain, qk_gain, window_blocks, w_spatial, w_temporal, w_out):
    rows_here, frames_here, _ = tokens.shape
    heads, width = qk_gain.shape[2:]
    ring = lax.axis_size("grp")
    me = lax.axis_index("grp")
    forward = [(i, (i + 1) % ring) for i in range(ring)]
    order = Order()

    def send(arrays):
        return [lax.ppermute(x, "grp", forward) for x in arrays]

    def swap(array):
        return lax.all_to_all(array, "seq", split_axis=0, concat_axis=0, tiled=True)

    wide = tokens.astype(jnp.float32)
    normed = (
        wide * lax.rsqrt(jnp.mean(wide * wide, axis=-1, keepdims=True) + EPS) * norm_gain
    ).astype(jnp.bfloat16)
    full_qkv = lax.all_gather(
        jnp.concatenate([w_spatial.transpose(1, 0, 2), w_temporal.transpose(1, 0, 2)]),
        "seq",
        axis=0,
    )
    full_out = lax.all_gather(w_out.transpose(1, 0, 2), "seq", axis=0)
    gains = jnp.concatenate([qk_gain, jnp.ones_like(qk_gain[:, :1])], axis=1)
    gains = gains * jnp.array([width**-0.5, 1.0, 1.0], jnp.float32)[None, :, None, None]
    gains = gains[:, :, :, None, :]
    table = slot_order(window_blocks, me, ring, rows_here // TILE)

    def temporal(k):
        (packed,) = project(order, [(TEMPORAL, [chunks[k]])], full_qkv, gains)
        exchanged[k] = swap(packed)

    def attend(k, ordered=False):
        temporal_outs[k] = swap(temporal_attention(order, exchanged[k], heads, ordered))

    def spatial(ks):
        tasks = [(SPATIAL, [chunks[k] for k in ks])]
        slots.update(zip(ks, project(order, tasks, full_qkv, gains)[0]))

    def finish(slot, frame, arrived, ordered=False):
        return finish_block(
            order,
            slot,
            frame,
            [slots[k][frame] for k in range(ring)],
            temporal_outs[slot],
            full_out,
            table,
            arrived,
            heads,
            ordered,
        )

    last = ring - 1
    chunks = [[normed[:, f] for f in range(frames_here)]]
    chunks += [[None] * frames_here for _ in range(last)]
    slots, exchanged, temporal_outs, arrived, sums = {}, {}, {}, {}, []
    for window in range(last + frames_here - 1):
        if arrived:
            for (k, f), x in zip(arrived, relay(order, list(arrived.values()))):
                chunks[k][f] = x
        steps = [window + 1 - f for f in range(frames_here)]
        moving = [(k, f) for f, k in enumerate(steps) if 1 <= k <= last]
        arrived = {(k, f): send([chunks[k - 1][f]])[0] for k, f in moving}
        ready = window - frames_here + 1
        if ready == 1 and last > 1:
            temporal(1)
            ahead = chunks[2][: frames_here - 1] if last > 2 else []
            groups = [chunks[1], chunks[0]] + ([ahead] if ahead else [])
            found = project(order, [(SPATIAL, groups)], full_qkv, gains)[0]
            slots[1], slots[0] = found[:2]
            if ahead:
                slots[2] = found[2]
            temporal(0)
            attend(1, True)
        elif ready > 0:
            at_end = ready == last - 1
            some = chunks[last][:-1] if at_end and frames_here > 1 else []
            have = slots.setdefault(ready, [])
            tasks = [
                (SPATIAL, [chunks[ready][len(have) :]] + ([some] if some else [])),
                (TEMPORAL, [chunks[ready]]),
            ]
            found = project(order, tasks, full_qkv, gains)
            slots[ready], exchanged[ready] = have + found[0][0], swap(found[1])
            if some:
                slots[last] = found[0][1]
                sums = [finish(1, f, None, True) for f in range(len(some))]
    for (k, f), x in arrived.items():
        chunks[k][f] = x
    if last == 1:
        temporal(1)
        spatial([0])
        temporal(0)
        attend(1, True)
    have = slots.setdefault(last, [])
    tasks = [(SPATIAL, [chunks[last][len(have) :]])]
    if last > 1:
        tasks += [(TEMPORAL, [chunks[last]])]
    found = project(order, tasks, full_qkv, gains)
    have += found[0][0]
    if last > 1:
        exchanged[last] = swap(found[1])
    sums = send(sums + [finish(1, f, None, True) for f in range(len(sums), frames_here)])
    for k in range(1, ring):
        if k not in temporal_outs and k < last:
            attend(k, True)
    for k in range(ring):
        if k not in temporal_outs:
            attend(k)
    for slot in range(2, ring):
        sums = send([finish(slot, f, sums[f]) for f in range(frames_here)])
    own = [finish(0, f, None) for f in range(frames_here)]
    return combine(tokens, own, sums)


def solution(mesh):
    return jax.shard_map(
        body,
        mesh=mesh,
        in_specs=(
            P("grp", "seq", None),
            P(),
            P(None, None, "grp", None),
            P(),
            P("seq", None, "grp"),
            P("seq", None, "grp"),
            P("seq", None, "grp"),
        ),
        out_specs=P("grp", "seq", None),
        check_vma=False,
    )
```

```python
import itertools

import jax
import jax.numpy as jnp
from jax import lax
from jax.experimental import pallas as pl
from jax.experimental.pallas import tpu as pltpu
from jax.sharding import PartitionSpec as P

TILE = 128
PROJECT_WEIGHT, LIGHT_WEIGHT = 3, 10
EPS = 1e-06
VMEM_BYTES = 56 * 1024 * 1024
VMEM = pl.BlockSpec(memory_space=pltpu.VMEM)
ANY = pl.BlockSpec(memory_space=pl.ANY)
MARK = jax.ShapeDtypeStruct((8, 128), jnp.float32)


def params():
    return pltpu.CompilerParams(vmem_limit_bytes=VMEM_BYTES)


def dot_transposed(a, b):
    return lax.dot_general(a, b, (((1,), (1,)), ((), ())), preferred_element_type=jnp.float32)


class Order:
    def __init__(self):
        self.mark = None

    def call(self, kernel, operands, in_specs, out_specs, out_shape, flops, ordered=False, **more):
        count = len(operands)
        marked = ordered and self.mark is not None

        def run(*refs):
            rest = refs[count + marked :]
            kernel(*refs[:count], *rest[: len(out_shape)], *rest[len(out_shape) + ordered :])

        outs = pl.pallas_call(
            run,
            in_specs=in_specs + [ANY] * marked,
            out_specs=out_specs + [ANY] * ordered,
            out_shape=out_shape + [MARK] * ordered,
            compiler_params=params(),
            cost_estimate=pl.CostEstimate(flops=flops, bytes_accessed=0, transcendentals=0),
            **more,
        )(*operands, *([self.mark] * marked))
        if ordered:
            *outs, self.mark = outs
        return outs


def relay(order, arrays):
    return order.call(
        lambda *refs: None,
        arrays,
        [ANY] * len(arrays),
        [ANY] * len(arrays),
        [jax.ShapeDtypeStruct(x.shape, x.dtype) for x in arrays],
        0,
        ordered=True,
        input_output_aliases={i: i for i in range(len(arrays))},
        name="relay",
    )


SPATIAL, TEMPORAL = 0, 1


def project(order, tasks, weights, gains):
    arrays = []
    for _, groups in tasks:
        arrays += [x for group in groups for x in group if not any(x is y for y in arrays)]
    row_count, depth = arrays[0].shape
    split, _, _, columns = weights.shape
    heads, width = gains.shape[2], gains.shape[4]
    part = row_count // split
    together = max(1, min(heads, 256 // width))
    span = together * width

    def index(x):
        return [y is x for y in arrays].index(True)

    def branch_at(j):
        found = tasks[0][0]
        for t in range(1, len(tasks)):
            found = jnp.where(j >= 3 * t, tasks[t][0], found)
        return found

    out_shape, out_specs, writes = [], [], []
    for t, (branch, groups) in enumerate(tasks):

        def place(j, t=t):
            return jnp.clip(j - 3 * t, 0, 2)

        writes.append([])
        for g, group in enumerate(groups):
            frames = len(group)
            for f, x in enumerate(group):
                first = len(out_shape) + (f if branch == SPATIAL else 0)
                writes[-1].append((index(x), first, g, f))
            if branch == SPATIAL:
                out_shape += [jax.ShapeDtypeStruct((row_count, 3 * columns), jnp.bfloat16)] * frames
                out_specs += [
                    pl.BlockSpec((row_count, columns), lambda j, place=place: (0, place(j)))
                ] * frames
        if branch == TEMPORAL:
            whole = (split, len(groups), len(groups[0]), part, 3 * columns)
            out_shape.append(jax.ShapeDtypeStruct(whole, jnp.bfloat16))
            out_specs.append(
                pl.BlockSpec(
                    whole[:-1] + (columns,), lambda j, place=place: (0, 0, 0, 0, place(j))
                )
            )

    def kernel(*refs):
        row_refs, w_ref, gain_ref = refs[: len(arrays)], refs[len(arrays)], refs[len(arrays) + 1]
        out_refs = refs[len(arrays) + 2 :]
        step = pl.program_id(0)
        kind = step % 3

        def run(t):
            for start in range(0, heads, together):
                w = w_ref[:, :, start * width : start * width + span].reshape(depth, span)
                for source, target, g, f in writes[t]:
                    projected = jnp.dot(
                        row_refs[source][...], w, preferred_element_type=jnp.float32
                    )
                    for h in range(together):
                        one = projected[:, h * width : (h + 1) * width]
                        scale = lax.rsqrt(jnp.mean(one * one, axis=-1, keepdims=True) + EPS)
                        scale = jnp.where(kind < 2, scale, 1.0)
                        one = one * scale * gain_ref[start + h]
                        at = pl.ds((start + h) * width, width)
                        if tasks[t][0] == TEMPORAL:
                            out_refs[target][:, g, f, :, at] = one.reshape(split, part, width).astype(
                                jnp.bfloat16
                            )
                        else:
                            out_refs[target][:, at] = one.astype(jnp.bfloat16)

        for t in range(len(tasks)):
            if len(tasks) == 1:
                run(t)
            else:
                pl.when(step // 3 == t)(lambda t=t: run(t))

    outs = order.call(
        kernel,
        [*arrays, weights, gains],
        [pl.BlockSpec((row_count, depth), lambda j: (0, 0), pipeline_mode=pl.Buffered(1))]
        * len(arrays)
        + [
            pl.BlockSpec(
                (split, None, depth // split, columns),
                lambda j: (0, 3 * branch_at(j) + j % 3, 0, 0),
            ),
            pl.BlockSpec((None, None, heads, 1, width), lambda j: (branch_at(j), j % 3, 0, 0, 0)),
        ],
        out_specs,
        out_shape,
        6 * sum(map(len, writes)) * row_count * depth * columns * PROJECT_WEIGHT,
        ordered=True,
        grid=(3 * len(tasks),),
        name="project",
    )
    outs, found = list(outs), []
    for branch, groups in tasks:
        if branch == TEMPORAL:
            found.append(outs.pop(0))
        else:
            found.append([[outs.pop(0) for _ in group] for group in groups])
    return found


def temporal_attention(order, packed, heads, ordered):
    split, chunks, frames_each, patches, columns = packed.shape
    frames = split * frames_each
    width = columns // (3 * heads)
    group = min(patches, max(256 // frames, 8))
    unit = frames * group

    def kernel(x_ref, out_ref):
        row = lax.broadcasted_iota(jnp.int32, (unit, unit), 0)
        col = lax.broadcasted_iota(jnp.int32, (unit, unit), 1)
        seen = (row % group == col % group) & (col // group <= row // group)

        def read(c, first, kind, h):
            at = (kind * heads + h) * width
            piece = x_ref[:, c, :, first : first + group, at : at + width]
            if group % 16:
                return piece.astype(jnp.float32).reshape(unit, width).astype(jnp.bfloat16)
            return piece.reshape(unit, width)

        for c, first in itertools.product(range(chunks), range(0, patches, group)):
            for h in range(heads):
                q, k, v = (read(c, first, kind, h) for kind in range(3))
                scores = dot_transposed(q, k)
                scores = jnp.where(seen, scores, jnp.float32(-1e30))
                scores = jnp.exp(scores - jnp.max(scores, axis=-1, keepdims=True))
                total = jnp.sum(scores, axis=-1, keepdims=True)
                attended = jnp.dot(
                    scores.astype(jnp.bfloat16), v, preferred_element_type=jnp.float32
                )
                attended = (attended / total).reshape(split, frames_each, group, width)
                out_ref[:, c, :, first : first + group, h * width : (h + 1) * width] = (
                    attended.astype(jnp.bfloat16)
                )

    return order.call(
        kernel,
        [packed],
        [VMEM],
        [VMEM],
        [jax.ShapeDtypeStruct(packed.shape[:-1] + (heads * width,), jnp.bfloat16)],
        4 * unit * unit * width * heads * chunks * (patches // group) // LIGHT_WEIGHT,
        ordered=ordered,
        name="temporal_attention",
    )[0]


def finish_block(order, slot, frame, slots, temporal_out, w_out, table, arrived, heads, ordered):
    count = len(slots)
    row_count, columns = slots[0].shape
    columns //= 3
    width = columns // heads
    tiles_each = row_count // TILE
    listed = table.shape[1]
    split, _, depth, _ = w_out.shape
    part = temporal_out.shape[3]
    adds = arrived is not None

    def kernel(*refs):
        table_ref, slot_refs = refs[0], refs[1 : 1 + count]
        t_hbm, w_hbm = refs[1 + count], refs[2 + count]
        out_ref, q_ref, k_ref, v_ref, t_ref, w_ref, o_ref, sems = refs[3 + count + adds :][:8]

        copies = []

        def copy(source, target):
            copies.append(pltpu.make_async_copy(source, target, sems.at[len(copies)]))
            copies[-1].start()
            return copies[-1]

        first = [copy(slot_refs[slot].at[:, pl.ds(0, columns)], q_ref)]
        for s in range(count):
            at = pl.ds(s * row_count, row_count)
            first.append(copy(slot_refs[s].at[:, pl.ds(columns, columns)], k_ref.at[at]))
            first.append(copy(slot_refs[s].at[:, pl.ds(2 * columns, columns)], v_ref.at[at]))
        second = [copy(t_hbm.at[:, 0, frame], t_ref), copy(w_hbm, w_ref)]
        if adds:
            arrived_ref = refs[-1]
            second.append(copy(refs[3 + count], arrived_ref))
        for one in first:
            one.wait()
        for i in range(tiles_each):
            picks = [
                pl.ds(pl.multiple_of(table_ref[slot * tiles_each + i, j] * TILE, TILE), TILE)
                for j in range(listed)
            ]
            cuts = [pl.ds(h * width, width) for h in range(heads)]
            scores = [
                dot_transposed(
                    q_ref[pl.ds(i * TILE, TILE), at],
                    jnp.concatenate([k_ref[p, at] for p in picks], axis=0),
                )
                for at in cuts
            ]
            scores = [jnp.exp(x - jnp.max(x, axis=-1, keepdims=True)) for x in scores]
            totals = [jnp.sum(x, axis=-1, keepdims=True) for x in scores]
            for at, x, total in zip(cuts, scores, totals):
                v = jnp.concatenate([v_ref[p, at] for p in picks], axis=0)
                attended = jnp.dot(x.astype(jnp.bfloat16), v, preferred_element_type=jnp.float32)
                o_ref[pl.ds(i * TILE, TILE), at] = (attended / total).astype(jnp.bfloat16)
        for one in second:
            one.wait()
        spatial = o_ref[...]
        temporal = t_ref[...]
        if part % 16:
            temporal = temporal.astype(jnp.float32)
        temporal = temporal.reshape(row_count, columns).astype(jnp.bfloat16)
        for s in range(split):
            at = pl.ds(s * depth, depth)
            value = dot_transposed(spatial, w_ref[s, 0]) + dot_transposed(temporal, w_ref[s, 1])
            if adds:
                value += arrived_ref[:, at].astype(jnp.float32)
            out_ref[:, at] = value.astype(jnp.bfloat16)

    operands = [table, *slots, temporal_out, w_out] + [arrived] * adds
    held = (row_count, split * depth)
    scratch = [
        pltpu.VMEM((row_count, columns), jnp.bfloat16),
        pltpu.VMEM((count * row_count, columns), jnp.bfloat16),
        pltpu.VMEM((count * row_count, columns), jnp.bfloat16),
        pltpu.VMEM((split, part, columns), jnp.bfloat16),
        pltpu.VMEM((split, 2, depth, columns), jnp.bfloat16),
        pltpu.VMEM((row_count, columns), jnp.bfloat16),
        pltpu.SemaphoreType.DMA((2 * count + 4,)),
    ]
    return order.call(
        kernel,
        operands,
        [pl.BlockSpec(memory_space=pltpu.SMEM)] + [ANY] * (len(operands) - 1),
        [VMEM],
        [jax.ShapeDtypeStruct(held, jnp.bfloat16)],
        (4 * row_count * listed * TILE * columns + 4 * row_count * columns * split * depth)
        // LIGHT_WEIGHT,
        ordered=ordered,
        scratch_shapes=scratch + [pltpu.VMEM(held, jnp.bfloat16)] * adds,
        name="finish_block",
    )[0]


def combine(tokens, own, sums):
    row_count, frames, depth = tokens.shape
    block = min(row_count, 32)

    def kernel(t_ref, *refs):
        out_ref = refs[-1]
        for f in range(frames):
            total = refs[f][...].astype(jnp.float32) + refs[frames + f][...].astype(jnp.float32)
            out_ref[:, f, :] = (t_ref[:, f, :].astype(jnp.float32) + total).astype(jnp.bfloat16)

    rows = pl.BlockSpec((block, depth), lambda i: (i, 0))
    whole = pl.BlockSpec((block, frames, depth), lambda i: (i, 0, 0))
    return pl.pallas_call(
        kernel,
        grid=(row_count // block,),
        in_specs=[whole] + [rows] * (2 * frames),
        out_specs=whole,
        out_shape=jax.ShapeDtypeStruct(tokens.shape, tokens.dtype),
        compiler_params=params(),
        name="combine",
    )(tokens, *own, *sums)


def slot_order(window_blocks, me, ring, tiles_each):
    def renumber(tile):
        return (me - tile // tiles_each + ring) % ring * tiles_each + tile % tiles_each

    rows = renumber(jnp.arange(ring * tiles_each, dtype=jnp.int32))
    return renumber(window_blocks[rows])


def body(tokens, norm_gain, qk_gain, window_blocks, w_spatial, w_temporal, w_out):
    rows_here, frames_here, _ = tokens.shape
    heads, width = qk_gain.shape[2:]
    ring = lax.axis_size("grp")
    me = lax.axis_index("grp")
    forward = [(i, (i + 1) % ring) for i in range(ring)]
    order = Order()

    def send(arrays):
        return [lax.ppermute(x, "grp", forward) for x in arrays]

    def swap(array):
        return lax.all_to_all(array, "seq", split_axis=0, concat_axis=0, tiled=True)

    wide = tokens.astype(jnp.float32)
    normed = (
        wide * lax.rsqrt(jnp.mean(wide * wide, axis=-1, keepdims=True) + EPS) * norm_gain
    ).astype(jnp.bfloat16)
    full_qkv = lax.all_gather(
        jnp.concatenate([w_spatial.transpose(1, 0, 2), w_temporal.transpose(1, 0, 2)]),
        "seq",
        axis=0,
    )
    full_out = lax.all_gather(w_out.transpose(1, 0, 2), "seq", axis=0)
    gains = jnp.concatenate([qk_gain, jnp.ones_like(qk_gain[:, :1])], axis=1)
    gains = gains * jnp.array([width**-0.5, 1.0, 1.0], jnp.float32)[None, :, None, None]
    gains = gains[:, :, :, None, :]
    table = slot_order(window_blocks, me, ring, rows_here // TILE)

    def temporal(k):
        (packed,) = project(order, [(TEMPORAL, [chunks[k]])], full_qkv, gains)
        exchanged[k] = swap(packed)

    def attend(k, ordered=False):
        temporal_outs[k] = swap(temporal_attention(order, exchanged[k], heads, ordered))

    def spatial(ks):
        tasks = [(SPATIAL, [chunks[k] for k in ks])]
        slots.update(zip(ks, project(order, tasks, full_qkv, gains)[0]))

    def finish(slot, frame, arrived, ordered=False):
        return finish_block(
            order,
            slot,
            frame,
            [slots[k][frame] for k in range(ring)],
            temporal_outs[slot],
            full_out,
            table,
            arrived,
            heads,
            ordered,
        )

    last = ring - 1
    chunks = [[normed[:, f] for f in range(frames_here)]]
    chunks += [[None] * frames_here for _ in range(last)]
    slots, exchanged, temporal_outs, arrived, sums = {}, {}, {}, {}, []
    for window in range(last + frames_here - 1):
        if arrived:
            for (k, f), x in zip(arrived, relay(order, list(arrived.values()))):
                chunks[k][f] = x
        steps = [window + 1 - f for f in range(frames_here)]
        moving = [(k, f) for f, k in enumerate(steps) if 1 <= k <= last]
        arrived = {(k, f): send([chunks[k - 1][f]])[0] for k, f in moving}
        ready = window - frames_here + 1
        if ready == 1 and last > 1:
            temporal(1)
            ahead = chunks[2][: frames_here - 1] if last > 2 else []
            groups = [chunks[1], chunks[0]] + ([ahead] if ahead else [])
            found = project(order, [(SPATIAL, groups)], full_qkv, gains)[0]
            slots[1], slots[0] = found[:2]
            if ahead:
                slots[2] = found[2]
            temporal(0)
            attend(1, True)
        elif ready > 0:
            at_end = ready == last - 1
            some = chunks[last][:-1] if at_end and frames_here > 1 else []
            have = slots.setdefault(ready, [])
            tasks = [
                (SPATIAL, [chunks[ready][len(have) :]] + ([some] if some else [])),
                (TEMPORAL, [chunks[ready]]),
            ]
            found = project(order, tasks, full_qkv, gains)
            slots[ready], exchanged[ready] = have + found[0][0], swap(found[1])
            if some:
                slots[last] = found[0][1]
                sums = [finish(1, f, None, True) for f in range(len(some))]
    for (k, f), x in arrived.items():
        chunks[k][f] = x
    if last == 1:
        temporal(1)
        spatial([0])
        temporal(0)
        attend(1, True)
    have = slots.setdefault(last, [])
    tasks = [(SPATIAL, [chunks[last][len(have) :]])]
    if last > 1:
        tasks += [(TEMPORAL, [chunks[last]])]
    found = project(order, tasks, full_qkv, gains)
    have += found[0][0]
    if last > 1:
        exchanged[last] = swap(found[1])
    sums = send(sums + [finish(1, f, None, True) for f in range(len(sums), frames_here)])
    for k in range(1, ring):
        if k not in temporal_outs and k < last:
            attend(k, True)
    for k in range(ring):
        if k not in temporal_outs:
            attend(k)
    for slot in range(2, ring):
        sums = send([finish(slot, f, sums[f]) for f in range(frames_here)])
    own = [finish(0, f, None) for f in range(frames_here)]
    return combine(tokens, own, sums)


def solution(mesh):
    return jax.shard_map(
        body,
        mesh=mesh,
        in_specs=(
            P("grp", "seq", None),
            P(),
            P(None, None, "grp", None),
            P(),
            P("seq", None, "grp"),
            P("seq", None, "grp"),
            P("seq", None, "grp"),
        ),
        out_specs=P("grp", "seq", None),
        check_vma=False,
    )
```
